512 devices in a mesh: slab: 128 (over y, x, z_lo), row: 4 (over z_hi, core).
Axes of the slice: x: 4, y: 8, z: 8 (z_hi: 2, z_lo: 4; z = z_hi * 4 + z_lo), core: 2. Of those that a mesh axis runs over, the one named last changes fastest.
Arguments:
- volume: bfloat16 [128, 2048, 2048], P('row', 'slab'), may hold values from -3 to 3
- magnify: float32 [128], P('row'), as said below
- goal: float32 [2048, 2048], P('slab', 'row'), may hold values from -6 to 6
- live_pixels: int32 [2048, 2048], P('slab', 'row'), may hold values 0 or 1
Outputs:
- projection: float32 [2048, 2048], P('slab', 'row')
- backprojection: bfloat16 [128, 2048, 2048], P('row', 'slab')
The draws below stay inside these ranges and needn't reach their ends.
Inputs may be any that keep to these rules, and one draw needn't show every extreme that they name: magnify rises strictly with the plane index and lies between 1 - s and 1 + s with s = 29 / 1025.
All inputs are finite; a program needn't handle non-finite values. No bound on the sum of `live_pixels` on one device may be relied on, other than what follows from the above.
Results may differ from the reference program's by a relative error of at most 0.009.
Values may be sent and summed in bfloat16 or wider, within the bound.
No kernel may reach another device: no remote copies, remote signals or barrier semaphores. Data moves between devices by JAX's collectives and lax.ppermute only.
A program may use at most 64 MiB of HBM per device.

```python
import jax
import jax.numpy as jnp
from jax import lax

VC = 2048
DC = 2048
ZS = 16
REACH = 2
VZ = 2048
DR = 2048
NPL = 128


def draw_magnify(key, part):
    key = jax.random.fold_in(key, 5)
    spread = (REACH * ZS - 3.0) / (VZ / 2.0 + 1.0)
    planes = jnp.arange(NPL).astype(jnp.float32)
    offsets = jax.random.uniform(key, (NPL,), jnp.float32)
    fraction = (planes + 0.2 + 0.6 * offsets) / NPL
    return (1.0 - spread + 2.0 * spread * fraction).astype(jnp.float32)


def touch_ends(drawn, stream_key, least, top_value):
    index_at = [jax.random.randint(jax.random.fold_in(stream_key, axis), (), 0, length) for axis, length in enumerate(drawn.shape)]
    widest = drawn.shape.index(max(drawn.shape))
    beside = index_at[:widest] + [(index_at[widest] + 1) % drawn.shape[widest]] + index_at[widest + 1:]
    return drawn.at[tuple(index_at)].set(least).at[tuple(beside)].set(top_value)


def block_levels(rng, dims, cuts, smallest, high):
    gain = 1.0
    for position, shards_of in cuts:
        steps = jax.random.uniform(jax.random.fold_in(jax.random.fold_in(rng, 6), position), (shards_of,), jnp.float32, smallest / len(cuts), high / len(cuts))
        gain = gain * jnp.repeat(jnp.exp(steps), dims[position] // shards_of).reshape((-1,) + (1,) * (len(dims) - 1 - position))
    return gain


def scatter_about(key, extent, width, bound, pieces=(), kind=jnp.bfloat16):
    values = width * jax.random.normal(key, extent, jnp.float32)
    if pieces:
        values = values * block_levels(key, extent, pieces, -0.22, 0.18)
    return jnp.clip(values, -bound, bound).astype(kind)


def setup_inputs(seed: int = 0) -> dict:
    seeds = jax.random.split(jax.random.key(seed), 5)
    volume = scatter_about(seeds[0], (NPL, VZ, VC), 0.2, 3.0, ((0, 4), (1, 128)))
    magnify = draw_magnify(jax.random.fold_in(seeds[4], 71), 0)
    goal = scatter_about(seeds[2], (DR, DC), 1.0, 6.0, ((0, 128), (1, 4)), jnp.float32)
    live_pixels = touch_ends((jax.random.randint(seeds[3], (DR, DC), 0, 16) < 15).astype(jnp.int32), jax.random.fold_in(seeds[3], 1), 0, 1)
    return {"volume": volume, "magnify": magnify, "goal": goal, "live_pixels": live_pixels}


def column_table(factor):
    columns = jnp.arange(DC).astype(jnp.float32)
    samples = ((columns + 0.5) - DC / 2) / factor + (VC / 2 - 0.5)
    floor_pos = jnp.floor(samples)
    ceil_pos = floor_pos + 1.0
    weight_low = jnp.where((floor_pos >= 0) & (floor_pos < VC), jnp.maximum(0.0, 1.0 - jnp.abs(samples - floor_pos)), 0.0).astype(jnp.bfloat16)
    weight_high = jnp.where((ceil_pos >= 0) & (ceil_pos < VC), jnp.maximum(0.0, 1.0 - jnp.abs(samples - ceil_pos)), 0.0).astype(jnp.bfloat16)
    index_low = jnp.clip(floor_pos.astype(jnp.int32), 0, VC - 1)
    index_high = jnp.clip(ceil_pos.astype(jnp.int32), 0, VC - 1)
    return index_low, index_high, weight_low, weight_high


def row_table(factor):
    detector = jnp.arange(DR).astype(jnp.float32)
    samples = ((detector + 0.5) - DR / 2) / factor + (VZ / 2 - 0.5)
    floor_pos = jnp.floor(samples)
    ceil_pos = floor_pos + 1.0
    weight_low = jnp.where((floor_pos >= 0) & (floor_pos < VZ), jnp.maximum(0.0, 1.0 - jnp.abs(samples - floor_pos)), 0.0).astype(jnp.bfloat16)
    weight_high = jnp.where((ceil_pos >= 0) & (ceil_pos < VZ), jnp.maximum(0.0, 1.0 - jnp.abs(samples - ceil_pos)), 0.0).astype(jnp.bfloat16)
    index_low = jnp.clip(floor_pos.astype(jnp.int32), 0, VZ - 1)
    index_high = jnp.clip(ceil_pos.astype(jnp.int32), 0, VZ - 1)
    return index_low, index_high, weight_low, weight_high


def reference(volume, magnify, goal, live_pixels):
    def forward(accum, inputs):
        plane_data, factor = inputs
        col_low, col_high, colw_low, colw_high = column_table(factor)
        values = plane_data.astype(jnp.float32)
        resampled = (values[:, col_low] * colw_low.astype(jnp.float32)[None, :]
                     + values[:, col_high] * colw_high.astype(jnp.float32)[None, :])
        resampled = lax.optimization_barrier(resampled.astype(jnp.bfloat16)).astype(jnp.float32)
        row_low, row_high, roww_low, roww_high = row_table(factor)
        sampled = (resampled[row_low] * roww_low.astype(jnp.float32)[:, None]
                   + resampled[row_high] * roww_high.astype(jnp.float32)[:, None])
        return accum + sampled, None

    empty = jnp.zeros((DR, DC), jnp.float32)
    projection, _ = lax.scan(forward, empty, (volume, magnify))
    residual = ((projection - goal) * live_pixels.astype(jnp.float32)).astype(jnp.bfloat16)
    residual_vals = residual.astype(jnp.float32)

    def backward(factor):
        col_low, col_high, colw_low, colw_high = column_table(factor)
        row_low, row_high, roww_low, roww_high = row_table(factor)
        smeared = jnp.zeros((VZ, DC), jnp.float32)
        smeared = smeared.at[row_low].add(residual_vals * roww_low.astype(jnp.float32)[:, None])
        smeared = smeared.at[row_high].add(residual_vals * roww_high.astype(jnp.float32)[:, None])
        smeared = lax.optimization_barrier(smeared.astype(jnp.bfloat16)).astype(jnp.float32)
        result = jnp.zeros((VZ, VC), jnp.float32)
        result = result.at[:, col_low].add(smeared * colw_low.astype(jnp.float32)[None, :])
        result = result.at[:, col_high].add(smeared * colw_high.astype(jnp.float32)[None, :])
        return result.astype(jnp.bfloat16)

    backprojection = lax.map(backward, magnify)
    return projection, backprojection
```

```python
import functools

import jax
import jax.numpy as jnp
from jax import lax
from jax.experimental import pallas as pl
from jax.experimental.pallas import tpu as pltpu
from jax.sharding import PartitionSpec as P

REACH = 2
BLOCKS = 2 * REACH + 1
LANES = 128
GROUP = 8
MARGIN = 32
DEAD = 1e30

LANE_GATHER = lax.GatherDimensionNumbers(
    offset_dims=(),
    collapsed_slice_dims=(1,),
    start_index_map=(1,),
    operand_batching_dims=(0,),
    start_indices_batching_dims=(0,),
)


def pick(block, lanes):
    return lax.gather(
        block,
        lanes[..., None],
        LANE_GATHER,
        (1, 1),
        mode=lax.GatherScatterMode.PROMISE_IN_BOUNDS,
    )


def pick_two(first, second, where_from):
    lanes = where_from & (LANES - 1)
    return jnp.where(where_from >= LANES, pick(second, lanes), pick(first, lanes))


def shifted(block, axis, distance):
    devices = range(lax.axis_size(axis))
    route = [(i - distance, i) for i in devices if i - distance in devices]
    return lax.ppermute(block, axis, route)


def factors_on_sublanes(magnify_ref, first):
    plane = lax.broadcasted_iota(jnp.int32, (GROUP, LANES), 0)
    factors = jnp.full((GROUP, LANES), magnify_ref[first], jnp.float32)
    for i in range(1, GROUP):
        factors = jnp.where(plane == i, magnify_ref[first + i], factors)
    return factors


def rounded(weights):
    return weights.astype(jnp.bfloat16).astype(jnp.float32)


def forward_kernel(
    place_ref, magnify_ref, volume_ref, own_ref, m2_ref, m1_ref, p1_ref, p2_ref,
    resampled, row_table, source, low, high,
):
    group = pl.program_id(0)
    first = group * GROUP
    slab_rows = volume_ref.shape[1]
    cols = volume_ref.shape[2]
    half = cols // 2
    blocks = cols // LANES
    frame_rows = BLOCKS * slab_rows
    rows_half = place_ref[1]

    factors = factors_on_sublanes(magnify_ref, first)
    shrinks = factors < 1.0
    lane = lax.broadcasted_iota(jnp.int32, (GROUP, LANES), 1)
    for b in range(blocks):
        column = (lane + b * LANES).astype(jnp.float32)
        at = (column + 0.5 - half) / factors + (half - 0.5)
        floor_at = jnp.floor(at)
        part = at - floor_at
        lower = max(b - 1, 0)
        upper = min(b, blocks - 2)
        if b < blocks // 2:
            base = jnp.where(shrinks, lower, upper)
        else:
            base = jnp.where(shrinks, upper, lower)
        position = floor_at.astype(jnp.int32)
        here = slice(b * LANES, (b + 1) * LANES)
        source[:, 0, here] = position - base * LANES
        low[:, 0, here] = jnp.where(
            (position >= 0) & (position < cols), rounded(1.0 - part), 0.0
        )
        high[:, 0, here] = jnp.where(
            (position >= -1) & (position < cols - 1), rounded(part), 0.0
        )

    row = lax.broadcasted_iota(jnp.int32, (frame_rows, GROUP * slab_rows), 0)
    lane_id = lax.broadcasted_iota(jnp.int32, (frame_rows, GROUP * slab_rows), 1)
    lane_factor = jnp.full((frame_rows, GROUP * slab_rows), magnify_ref[first], jnp.float32)
    for i in range(1, GROUP):
        lane_factor = jnp.where(lane_id >= i * slab_rows, magnify_ref[first + i], lane_factor)
    middle = rows_half.astype(jnp.float32)
    detector = (row + (place_ref[0] - REACH * slab_rows)).astype(jnp.float32)
    sample = (detector + 0.5 - middle) / lane_factor + (middle - 0.5)
    axial = (lane_id % slab_rows + place_ref[0]).astype(jnp.float32)
    row_table[:, pl.ds(pl.multiple_of(group * GROUP * slab_rows, LANES), GROUP * slab_rows)] = (
        jnp.maximum(0.0, 1.0 - jnp.abs(sample - axial)).astype(jnp.bfloat16)
    )

    def plane_step(i, carry):
        shrink = (magnify_ref[first + i] < 1.0).astype(jnp.int32)
        out_row = pl.multiple_of((first + i) * slab_rows, slab_rows)
        for b in range(blocks):
            here = slice(b * LANES, (b + 1) * LANES)
            if b < blocks // 2:
                base = jnp.maximum(b - shrink, 0)
            else:
                base = jnp.minimum(b - 1 + shrink, blocks - 2)
            start = pl.multiple_of(base * LANES, LANES)
            one = volume_ref[i, :, pl.ds(start, LANES)]
            two = volume_ref[i, :, pl.ds(start + LANES, LANES)]
            where_from = jnp.broadcast_to(source[i, :, here], (slab_rows, LANES))
            at_low = pick_two(one, two, where_from.astype(jnp.int16))
            at_high = pick_two(one, two, (where_from + 1).astype(jnp.int16))
            value = at_low.astype(jnp.float32) * low[i, :, here] + at_high.astype(
                jnp.float32
            ) * high[i, :, here]
            resampled[pl.ds(out_row, slab_rows), here] = value.astype(jnp.bfloat16)
        return carry

    lax.fori_loop(0, GROUP, plane_step, 0)

    @pl.when(group == pl.num_programs(0) - 1)
    def _():
        for c in range(0, cols, 512):
            frame = jnp.dot(
                row_table[...], resampled[:, c : c + 512], preferred_element_type=jnp.float32
            )
            for position, ref in enumerate((m2_ref, m1_ref, own_ref, p1_ref, p2_ref)):
                ref[:, c : c + 512] = frame[
                    position * slab_rows : (position + 1) * slab_rows
                ].astype(ref.dtype)


def backward_kernel(
    place_ref, magnify_ref, m2_ref, m1_ref, own_ref, p1_ref, p2_ref, out_ref,
    frame, row_table, smeared, source, weight0, weight1, weight2,
):
    group = pl.program_id(0)
    first = group * GROUP
    slab_rows = out_ref.shape[1]
    cols = out_ref.shape[2]
    half = cols // 2
    blocks = cols // LANES
    rows_half = place_ref[1]

    @pl.when(group == 0)
    def _():
        frame[BLOCKS * slab_rows :, :] = jnp.zeros(
            (frame.shape[0] - BLOCKS * slab_rows, frame.shape[1]), frame.dtype
        )
        for position, ref in enumerate((m2_ref, m1_ref, own_ref, p1_ref, p2_ref)):
            values = ref[...].astype(jnp.float32)
            padded = jnp.concatenate(
                [values, jnp.zeros((slab_rows, LANES), jnp.float32)], axis=1
            )
            frame[position * slab_rows : (position + 1) * slab_rows, :] = pltpu.roll(
                padded, MARGIN, 1
            ).astype(frame.dtype)

    factors = factors_on_sublanes(magnify_ref, first)
    lane = lax.broadcasted_iota(jnp.int32, (GROUP, LANES), 1)
    for b in range(blocks):
        target = (lane + b * LANES).astype(jnp.float32)
        reach = (target - (half + 0.5)) * factors + (half - 0.501)
        tap = jnp.floor(reach) + 1.0
        here = slice(b * LANES, (b + 1) * LANES)
        source[:, 0, here] = tap.astype(jnp.int32) + (MARGIN - b * LANES)
        for step, weight in enumerate((weight0, weight1, weight2)):
            at = (tap + (step + 0.5 - half)) / factors + (half - 0.5)
            weight[:, 0, here] = rounded(jnp.maximum(0.0, 1.0 - jnp.abs(at - target)))

    middle = rows_half.astype(jnp.float32)
    row = lax.broadcasted_iota(jnp.int32, (slab_rows, LANES), 0)
    lane_id = lax.broadcasted_iota(jnp.int32, (slab_rows, LANES), 1)
    axial = (row + place_ref[0]).astype(jnp.float32)
    detector = (lane_id + (place_ref[0] - REACH * slab_rows)).astype(jnp.float32)
    for i in range(GROUP):
        sample = (detector + 0.5 - middle) / magnify_ref[first + i] + (middle - 0.5)
        row_table[i * slab_rows : (i + 1) * slab_rows, :] = jnp.maximum(
            0.0, 1.0 - jnp.abs(sample - axial)
        ).astype(jnp.bfloat16)
    smeared[...] = jnp.dot(
        row_table[...], frame[...], preferred_element_type=jnp.float32
    ).astype(jnp.bfloat16)

    def plane_step(i, carry):
        in_row = pl.multiple_of(i * slab_rows, slab_rows)
        for b in range(blocks):
            here = slice(b * LANES, (b + 1) * LANES)
            one = smeared[pl.ds(in_row, slab_rows), here]
            two = smeared[pl.ds(in_row, slab_rows), (b + 1) * LANES : (b + 2) * LANES]
            where_from = jnp.broadcast_to(source[i, :, here], (slab_rows, LANES))
            value = None
            for step, weight in enumerate((weight0, weight1, weight2)):
                term = pick_two(one, two, (where_from + step).astype(jnp.int16)).astype(
                    jnp.float32
                ) * weight[i, :, here]
                value = term if value is None else value + term
            out_ref[i, :, here] = value.astype(out_ref.dtype)
        return carry

    lax.fori_loop(0, GROUP, plane_step, 0)


def whole(shape):
    return pl.BlockSpec(shape, lambda g: (0,) * len(shape))


def forward(place, magnify, volume):
    planes, slab_rows, cols = volume.shape
    band = (slab_rows, cols)
    return pl.pallas_call(
        forward_kernel,
        grid=(planes // GROUP,),
        in_specs=[
            pl.BlockSpec(memory_space=pltpu.SMEM),
            pl.BlockSpec(memory_space=pltpu.SMEM),
            pl.BlockSpec((GROUP, slab_rows, cols), lambda g: (g, 0, 0)),
        ],
        out_specs=[whole(band)] * BLOCKS,
        out_shape=[jax.ShapeDtypeStruct(band, jnp.float32)]
        + [jax.ShapeDtypeStruct(band, jnp.bfloat16)] * (BLOCKS - 1),
        scratch_shapes=[
            pltpu.VMEM((planes * slab_rows, cols), jnp.bfloat16),
            pltpu.VMEM((BLOCKS * slab_rows, planes * slab_rows), jnp.bfloat16),
            pltpu.VMEM((GROUP, 1, cols), jnp.int32),
            pltpu.VMEM((GROUP, 1, cols), jnp.float32),
            pltpu.VMEM((GROUP, 1, cols), jnp.float32),
        ],
        compiler_params=pltpu.CompilerParams(
            dimension_semantics=("arbitrary",), vmem_limit_bytes=32 << 20
        ),
        name="forward_planes",
    )(place, magnify, volume)


def backward(place, magnify, bands):
    planes = magnify.shape[0]
    slab_rows, cols = bands[0].shape
    return pl.pallas_call(
        backward_kernel,
        grid=(planes // GROUP,),
        in_specs=[
            pl.BlockSpec(memory_space=pltpu.SMEM),
            pl.BlockSpec(memory_space=pltpu.SMEM),
        ]
        + [whole((slab_rows, cols))] * BLOCKS,
        out_specs=pl.BlockSpec((GROUP, slab_rows, cols), lambda g: (g, 0, 0)),
        out_shape=jax.ShapeDtypeStruct((planes, slab_rows, cols), jnp.bfloat16),
        scratch_shapes=[
            pltpu.VMEM((LANES, cols + LANES), jnp.bfloat16),
            pltpu.VMEM((GROUP * slab_rows, LANES), jnp.bfloat16),
            pltpu.VMEM((GROUP * slab_rows, cols + LANES), jnp.bfloat16),
            pltpu.VMEM((GROUP, 1, cols), jnp.int32),
            pltpu.VMEM((GROUP, 1, cols), jnp.float32),
            pltpu.VMEM((GROUP, 1, cols), jnp.float32),
            pltpu.VMEM((GROUP, 1, cols), jnp.float32),
        ],
        compiler_params=pltpu.CompilerParams(
            dimension_semantics=("arbitrary",), vmem_limit_bytes=32 << 20
        ),
        name="backward_planes",
    )(place, magnify, *bands)


def shards(volume, magnify, goal, live_pixels):
    slab_rows, own_cols = goal.shape
    row_count = lax.axis_size("row")
    cols = own_cols * row_count
    rows_all = slab_rows * lax.axis_size("slab")
    vol_first = lax.axis_index("slab") * slab_rows
    place = jnp.stack([vol_first, jnp.int32(rows_all // 2)]).astype(jnp.int32)

    own, m2, m1, p1, p2 = forward(place, magnify, volume)
    arrived = [
        shifted(block, "slab", distance)
        for block, distance in ((m1, -1), (p1, 1), (m2, -2), (p2, 2))
    ]
    total = own
    for block in arrived:
        total = total + block.astype(jnp.float32)

    coarse = goal.astype(jnp.bfloat16)
    fine = (goal - coarse.astype(jnp.float32)).astype(jnp.bfloat16)
    coarse = jnp.where(live_pixels == 0, jnp.bfloat16(DEAD), coarse)
    message = jnp.concatenate([total.astype(jnp.bfloat16), coarse, fine], axis=1)
    gathered = lax.all_gather(message, "row", axis=0, tiled=False).astype(jnp.float32)
    projection = gathered[:, :, :cols].sum(axis=0)
    all_coarse = jnp.concatenate(
        [gathered[r, :, cols : cols + own_cols] for r in range(row_count)], axis=1
    )
    all_fine = jnp.concatenate(
        [gathered[r, :, cols + own_cols :] for r in range(row_count)], axis=1
    )
    residual = jnp.where(
        all_coarse > 0.5 * DEAD, 0.0, projection - (all_coarse + all_fine)
    ).astype(jnp.bfloat16)
    own_projection = lax.dynamic_slice_in_dim(
        projection, lax.axis_index("row") * own_cols, own_cols, axis=1
    )

    n1, q1, n2, q2 = (shifted(residual, "slab", d) for d in (-1, 1, -2, 2))
    backprojection = backward(place, magnify, (q2, q1, residual, n1, n2))
    return (own_projection, backprojection)


def solution(mesh):
    in_specs = (P("row", "slab", None), P("row"), P("slab", "row"), P("slab", "row"))
    out_specs = (P("slab", "row"), P("row", "slab", None))
    return jax.shard_map(shards, mesh=mesh, in_specs=in_specs, out_specs=out_specs, check_vma=False)
```

```python
import jax
import jax.numpy as jnp
from jax import lax
from jax.experimental import pallas as pl
from jax.experimental.pallas import tpu as pltpu
from jax.sharding import PartitionSpec as P

REACH = 2
BLOCKS = 2 * REACH + 1
LANES = 128
GROUP = 8
RUN = 121
DEAD = 1e30

LANE_GATHER = lax.GatherDimensionNumbers(
    offset_dims=(),
    collapsed_slice_dims=(1,),
    start_index_map=(1,),
    operand_batching_dims=(0,),
    start_indices_batching_dims=(0,),
)


def pick(block, lanes):
    return lax.gather(
        block,
        lanes[..., None],
        LANE_GATHER,
        (1, 1),
        mode=lax.GatherScatterMode.PROMISE_IN_BOUNDS,
    )


def window(start, ref, rows, last):
    block = start // LANES
    one = ref[rows + (pl.ds(pl.multiple_of(block * LANES, LANES), LANES),)]
    following = jnp.minimum(block + 1, last)
    two = ref[rows + (pl.ds(pl.multiple_of(following * LANES, LANES), LANES),)]
    lane = lax.broadcasted_iota(jnp.int32, one.shape, 1).astype(jnp.int16)
    edge = jnp.full(one.shape, start % LANES, jnp.int32).astype(jnp.int16)
    return jnp.where(lane >= edge, one, two)


def joined(group, before, after):
    lane = lax.broadcasted_iota(jnp.int32, before.shape, 1).astype(jnp.int16)
    return jnp.where(lane < RUN - (LANES - RUN) * group, before, after)


def run_columns(group, lane):
    return lane + jnp.where(lane >= LANES - (LANES - RUN) * group, group - 1, group) * LANES


def whole_start(position, last):
    return jnp.clip(position, 0.0, last).astype(jnp.int32)


def factors_on_sublanes(magnify_ref, first):
    plane = lax.broadcasted_iota(jnp.int32, (GROUP, LANES), 0)
    factors = jnp.full((GROUP, LANES), magnify_ref[first], jnp.float32)
    for i in range(1, GROUP):
        factors = jnp.where(plane == i, magnify_ref[first + i], factors)
    return factors


def rounded(weights):
    return weights.astype(jnp.bfloat16).astype(jnp.float32)


def forward_kernel(
    magnify_ref, volume_ref, own_ref, near_ref, far_ref, send_ref,
    resampled, row_table, source, low, high,
):
    group = pl.program_id(0)
    first = group * GROUP
    slab_rows = volume_ref.shape[1]
    cols = volume_ref.shape[2]
    half = cols // 2
    blocks = cols // LANES
    frame_rows = BLOCKS * slab_rows
    vol_first = lax.axis_index("slab") * slab_rows
    middle = slab_rows * lax.axis_size("slab") // 2

    factors = factors_on_sublanes(magnify_ref, first)
    lane = lax.broadcasted_iota(jnp.int32, (GROUP, LANES), 1)
    for g in range(blocks + 1):
        column = run_columns(g, lane).astype(jnp.float32)
        at = (column + 0.5 - half) / factors + (half - 0.5)
        floor_at = jnp.floor(at)
        part = at - floor_at
        position = floor_at.astype(jnp.int32)
        here = slice(g * LANES, (g + 1) * LANES)
        source[:, here] = position & (LANES - 1)
        low[:, here] = jnp.where(
            (position >= 0) & (position < cols), rounded(1.0 - part), 0.0
        )
        high[:, here] = jnp.where(
            (position >= -1) & (position < cols - 1), rounded(part), 0.0
        )

    row = lax.broadcasted_iota(jnp.int32, (frame_rows, GROUP * slab_rows), 0)
    lane_id = lax.broadcasted_iota(jnp.int32, (frame_rows, GROUP * slab_rows), 1)
    lane_factor = jnp.full((frame_rows, GROUP * slab_rows), magnify_ref[first], jnp.float32)
    for i in range(1, GROUP):
        lane_factor = jnp.where(lane_id >= i * slab_rows, magnify_ref[first + i], lane_factor)
    detector = (row + (vol_first - REACH * slab_rows)).astype(jnp.float32)
    sample = (detector + (0.5 - middle)) / lane_factor + (middle - 0.5)
    axial = (lane_id % slab_rows + vol_first).astype(jnp.float32)
    row_table[:, pl.ds(pl.multiple_of(group * GROUP * slab_rows, LANES), GROUP * slab_rows)] = (
        jnp.maximum(0.0, 1.0 - jnp.abs(sample - axial)).astype(jnp.bfloat16)
    )

    for i in range(GROUP):
        rate = 1.0 / magnify_ref[first + i]
        out_row = pl.multiple_of((first + i) * slab_rows, slab_rows)
        before = None
        for g in range(blocks + 1):
            here = slice(g * LANES, (g + 1) * LANES)
            start = whole_start(
                (g * RUN + 0.5 - half) * rate + (half - 0.75), float(cols - LANES)
            )
            values = window(start, volume_ref, (i, slice(None)), blocks - 1)
            lanes = jnp.broadcast_to(source[i : i + 1, here], values.shape).astype(jnp.int16)
            at_low = pick(values, lanes).astype(jnp.float32)
            at_high = pick(values, (lanes + 1) & (LANES - 1)).astype(jnp.float32)
            run = (at_low * low[i : i + 1, here] + at_high * high[i : i + 1, here]).astype(
                jnp.bfloat16
            )
            if before is not None:
                resampled[pl.ds(out_row, slab_rows), (g - 1) * LANES : g * LANES] = joined(
                    g - 1, before, run
                )
            before = run

    @pl.when(group == pl.num_programs(0) - 1)
    def _():
        upward = lax.axis_index("row") % 2 == 0
        r = slab_rows
        for c in range(0, cols, 512):
            here = slice(c, c + 512)
            frame = jnp.dot(
                row_table[...], resampled[:, here], preferred_element_type=jnp.float32
            )
            own_ref[:, here] = frame[2 * r : 3 * r]
            near_ref[:, here] = jnp.where(upward, frame[3 * r : 4 * r], frame[r : 2 * r])
            far_ref[:, here] = jnp.where(upward, frame[4 * r :], frame[:r])
            send_ref[:r, here] = jnp.where(upward, frame[r : 2 * r], frame[3 * r : 4 * r]).astype(
                send_ref.dtype
            )
            send_ref[r:, here] = jnp.where(upward, frame[:r], frame[4 * r :]).astype(
                send_ref.dtype
            )


def backward_kernel(
    magnify_ref, own_ref, halo_ref, out_ref,
    frame, row_table, smeared, source, weight0, weight1, weight2,
):
    group = pl.program_id(0)
    first = group * GROUP
    slab_rows = out_ref.shape[1]
    cols = out_ref.shape[2]
    half = cols // 2
    blocks = cols // LANES
    vol_first = lax.axis_index("slab") * slab_rows
    middle = slab_rows * lax.axis_size("slab") // 2

    @pl.when(group == 0)
    def _():
        r = slab_rows
        frame[:r, :] = halo_ref[0, r:, :]
        frame[r : 2 * r, :] = halo_ref[0, :r, :]
        frame[2 * r : 3 * r, :] = own_ref[...]
        frame[3 * r : 5 * r, :] = halo_ref[1]
        frame[5 * r :, :] = jnp.zeros((frame.shape[0] - 5 * r, cols), frame.dtype)

    factors = factors_on_sublanes(magnify_ref, first)
    lane = lax.broadcasted_iota(jnp.int32, (GROUP, LANES), 1)
    for g in range(blocks + 1):
        target = run_columns(g, lane).astype(jnp.float32)
        tap = jnp.floor((target - (half + 0.5)) * factors + (half - 0.501)) + 1.0
        here = slice(g * LANES, (g + 1) * LANES)
        source[:, here] = tap.astype(jnp.int32) & (LANES - 1)
        for step, weight in enumerate((weight0, weight1, weight2)):
            column = tap + step
            at = (column + (0.5 - half)) / factors + (half - 0.5)
            weight[:, here] = jnp.where(
                (column >= 0.0) & (column < cols),
                rounded(jnp.maximum(0.0, 1.0 - jnp.abs(at - target))),
                0.0,
            )

    row = lax.broadcasted_iota(jnp.int32, (slab_rows, LANES), 0)
    lane_id = lax.broadcasted_iota(jnp.int32, (slab_rows, LANES), 1)
    axial = (row + vol_first).astype(jnp.float32)
    detector = (lane_id + (vol_first - REACH * slab_rows)).astype(jnp.float32)
    for i in range(GROUP):
        sample = (detector + (0.5 - middle)) / magnify_ref[first + i] + (middle - 0.5)
        row_table[i * slab_rows : (i + 1) * slab_rows, :] = jnp.maximum(
            0.0, 1.0 - jnp.abs(sample - axial)
        ).astype(jnp.bfloat16)
    smeared[...] = jnp.dot(
        row_table[...], frame[...], preferred_element_type=jnp.float32
    ).astype(jnp.bfloat16)

    for i in range(GROUP):
        factor = magnify_ref[first + i]
        rows = (slice(i * slab_rows, (i + 1) * slab_rows),)
        before = None
        for g in range(blocks + 1):
            here = slice(g * LANES, (g + 1) * LANES)
            start = whole_start(
                (g * RUN - (half + 0.5)) * factor + (half + 0.249), float(cols - LANES)
            )
            values = window(start, smeared, rows, blocks - 1)
            lanes = jnp.broadcast_to(source[i : i + 1, here], values.shape).astype(jnp.int16)
            total = pick(values, lanes).astype(jnp.float32) * weight0[i : i + 1, here]
            for step, weight in ((1, weight1), (2, weight2)):
                total = total + pick(values, (lanes + step) & (LANES - 1)).astype(
                    jnp.float32
                ) * weight[i : i + 1, here]
            run = total.astype(out_ref.dtype)
            if before is not None:
                out_ref[i, :, (g - 1) * LANES : g * LANES] = joined(g - 1, before, run)
            before = run


def whole(shape):
    return pl.BlockSpec(shape, lambda g: (0,) * len(shape))


PARAMS = pltpu.CompilerParams(dimension_semantics=("arbitrary",), vmem_limit_bytes=56 << 20)


def forward(magnify, volume):
    planes, slab_rows, cols = volume.shape
    band = (slab_rows, cols)
    pair = (2 * slab_rows, cols)
    run_cols = cols + LANES
    return pl.pallas_call(
        forward_kernel,
        grid=(planes // GROUP,),
        in_specs=[
            pl.BlockSpec(memory_space=pltpu.SMEM),
            pl.BlockSpec((GROUP, slab_rows, cols), lambda g: (g, 0, 0)),
        ],
        out_specs=[whole(band)] * 3 + [whole(pair)],
        out_shape=[jax.ShapeDtypeStruct(band, jnp.float32)] * 3
        + [jax.ShapeDtypeStruct(pair, jnp.bfloat16)],
        scratch_shapes=[
            pltpu.VMEM((planes * slab_rows, cols), jnp.bfloat16),
            pltpu.VMEM((BLOCKS * slab_rows, planes * slab_rows), jnp.bfloat16),
            pltpu.VMEM((GROUP, run_cols), jnp.int32),
            pltpu.VMEM((GROUP, run_cols), jnp.float32),
            pltpu.VMEM((GROUP, run_cols), jnp.float32),
        ],
        compiler_params=PARAMS,
        name="forward_planes",
    )(magnify, volume)


def backward(magnify, residual, halo):
    planes = magnify.shape[0]
    slab_rows, cols = residual.shape
    run_cols = cols + LANES
    return pl.pallas_call(
        backward_kernel,
        grid=(planes // GROUP,),
        in_specs=[
            pl.BlockSpec(memory_space=pltpu.SMEM),
            whole(residual.shape),
            whole(halo.shape),
        ],
        out_specs=pl.BlockSpec((GROUP, slab_rows, cols), lambda g: (g, 0, 0)),
        out_shape=jax.ShapeDtypeStruct((planes, slab_rows, cols), jnp.bfloat16),
        scratch_shapes=[
            pltpu.VMEM((LANES, cols), jnp.bfloat16),
            pltpu.VMEM((GROUP * slab_rows, LANES), jnp.bfloat16),
            pltpu.VMEM((GROUP * slab_rows, cols), jnp.bfloat16),
            pltpu.VMEM((GROUP, run_cols), jnp.int32),
            pltpu.VMEM((GROUP, run_cols), jnp.float32),
            pltpu.VMEM((GROUP, run_cols), jnp.float32),
            pltpu.VMEM((GROUP, run_cols), jnp.float32),
        ],
        compiler_params=PARAMS,
        name="backward_planes",
    )(magnify, residual, halo)


def both_ways(block, distance):
    slabs, members = lax.axis_size("slab"), lax.axis_size("row")
    route = []
    for s in range(slabs):
        for q in range(members):
            to = s + (distance if q % 2 == 0 else -distance)
            if 0 <= to < slabs:
                route.append((s * members + q, to * members + q))
    return lax.ppermute(block, ("slab", "row"), route)


def shards(volume, magnify, goal, live_pixels):
    slab_rows, own_cols = goal.shape
    row_count = lax.axis_size("row")
    cols = own_cols * row_count

    own, near, far, send = forward(magnify, volume)
    got = lax.ppermute(send, "row", [(q, q ^ 1) for q in range(row_count)]).astype(jnp.float32)
    near = both_ways((near + got[:slab_rows]).astype(jnp.bfloat16), 1)
    far = both_ways((far + got[slab_rows:]).astype(jnp.bfloat16), 2)
    total = own + near.astype(jnp.float32) + far.astype(jnp.float32)

    coarse = goal.astype(jnp.bfloat16)
    fine = (goal - coarse.astype(jnp.float32)).astype(jnp.bfloat16)
    coarse = jnp.where(live_pixels == 0, jnp.bfloat16(DEAD), coarse)
    message = jnp.concatenate([total.astype(jnp.bfloat16), coarse, fine], axis=1)
    gathered = lax.all_gather(message, "row", axis=0, tiled=False).astype(jnp.float32)
    projection = gathered[:, :, :cols].sum(axis=0)
    all_coarse = jnp.concatenate(
        [gathered[r, :, cols : cols + own_cols] for r in range(row_count)], axis=1
    )
    all_fine = jnp.concatenate(
        [gathered[r, :, cols + own_cols :] for r in range(row_count)], axis=1
    )
    residual = jnp.where(
        all_coarse > 0.5 * DEAD, 0.0, projection - (all_coarse + all_fine)
    ).astype(jnp.bfloat16)
    own_projection = lax.dynamic_slice_in_dim(
        projection, lax.axis_index("row") * own_cols, own_cols, axis=1
    )

    arrived = jnp.concatenate([both_ways(residual, 1), both_ways(residual, 2)], axis=0)
    halo = lax.all_gather(
        arrived, "row", axis_index_groups=[[q, q + 1] for q in range(0, row_count, 2)]
    )
    return (own_projection, backward(magnify, residual, halo))


def solution(mesh):
    in_specs = (P("row", "slab", None), P("row"), P("slab", "row"), P("slab", "row"))
    out_specs = (P("slab", "row"), P("row", "slab", None))
    return jax.shard_map(shards, mesh=mesh, in_specs=in_specs, out_specs=out_specs, check_vma=False)
```

```python
import jax
import jax.numpy as jnp
from jax import lax
from jax.experimental import pallas as pl
from jax.experimental.pallas import tpu as pltpu
from jax.sharding import PartitionSpec as P

REACH = 2
BLOCKS = 2 * REACH + 1
LANES = 128
LANE_BITS = 7
FIXED_BITS = 16
FIXED = float(1 << FIXED_BITS)
GROUP = 8
SENT = 4
FETCHED = 8
CHIP_RUN = 4
RUN = 121
DEAD = 1e30

LANE_GATHER = lax.GatherDimensionNumbers(
    offset_dims=(),
    collapsed_slice_dims=(1,),
    start_index_map=(1,),
    operand_batching_dims=(0,),
    start_indices_batching_dims=(0,),
)


def pick(block, lanes):
    return lax.gather(
        block,
        lanes[..., None],
        LANE_GATHER,
        (1, 1),
        mode=lax.GatherScatterMode.PROMISE_IN_BOUNDS,
    )


def window(start, ref, rows):
    block = pl.multiple_of((start >> LANE_BITS) * LANES, LANES)
    one = ref[rows + (pl.ds(block, LANES),)]
    two = ref[rows + (pl.ds(block + LANES, LANES),)]
    lane = lax.broadcasted_iota(jnp.int32, one.shape, 1).astype(jnp.int16)
    edge = jnp.full(one.shape, start & (LANES - 1), jnp.int32).astype(jnp.int16)
    return jnp.where(lane >= edge, one, two)


def joined(group, before, after):
    lane = lax.broadcasted_iota(jnp.int32, before.shape, 1).astype(jnp.int16)
    return jnp.where(lane < RUN - (LANES - RUN) * group, before, after)


def run_columns(group, lane):
    return lane + jnp.where(lane >= LANES - (LANES - RUN) * group, group - 1, group) * LANES


def run_starts(first, stride, last):
    at = (first * FIXED).astype(jnp.int32)
    step = (stride * FIXED).astype(jnp.int32)
    while True:
        yield jnp.clip(at >> FIXED_BITS, 0, last)
        at = at + step


def factors_on_sublanes(magnify_ref, first):
    plane = lax.broadcasted_iota(jnp.int32, (GROUP, LANES), 0)
    factors = jnp.full((GROUP, LANES), magnify_ref[first], jnp.float32)
    for i in range(1, GROUP):
        factors = jnp.where(plane == i, magnify_ref[first + i], factors)
    return factors


def rounded(weights):
    return weights.astype(jnp.bfloat16).astype(jnp.float32)


def interpolated(values, lanes, weights):
    total = None
    for step, weight in enumerate(weights):
        picked = pick(values, (lanes + step) & (LANES - 1) if step else lanes)
        term = picked.astype(jnp.float32) * weight
        total = term if total is None else total + term
    return total.astype(values.dtype)


def forward_kernel(
    magnify_ref, volume_ref, own_ref, near_ref, far_ref, send_ref,
    volume, arrival, resampled, row_table, source, low, high,
):
    planes, slab_rows, cols = volume_ref.shape
    groups = planes // GROUP
    half = cols // 2
    blocks = cols // LANES
    frame_rows = BLOCKS * slab_rows
    vol_first = lax.axis_index("slab") * slab_rows
    middle = slab_rows * lax.axis_size("slab") // 2

    def fetch(part):
        planes_of = pl.ds(part * FETCHED, FETCHED)
        return pltpu.make_async_copy(
            volume_ref.at[planes_of], volume.at[planes_of, :, pl.ds(0, cols)], arrival.at[part]
        )

    for part in range(planes // FETCHED):
        fetch(part).start()

    lane = lax.broadcasted_iota(jnp.int32, (GROUP, LANES), 1)
    row = lax.broadcasted_iota(jnp.int32, (frame_rows, GROUP * slab_rows), 0)
    lane_id = lax.broadcasted_iota(jnp.int32, (frame_rows, GROUP * slab_rows), 1)
    detector = (row + (vol_first - REACH * slab_rows)).astype(jnp.float32) + (0.5 - middle)
    axial = ((lane_id & (slab_rows - 1)) + vol_first).astype(jnp.float32) - (middle - 0.5)

    def group_step(group, carry):
        first = group * GROUP
        factors = factors_on_sublanes(magnify_ref, first)
        for g in range(blocks + 1):
            column = run_columns(g, lane).astype(jnp.float32)
            at = (column + 0.5 - half) / factors + (half - 0.5)
            floor_at = jnp.floor(at)
            part = at - floor_at
            position = floor_at.astype(jnp.int32)
            here = slice(g * LANES, (g + 1) * LANES)
            source[:, here] = position & (LANES - 1)
            low[:, here] = jnp.where(
                (position >= 0) & (position < cols), rounded(1.0 - part), 0.0
            )
            high[:, here] = jnp.where(
                (position >= -1) & (position < cols - 1), rounded(part), 0.0
            )

        lane_factor = jnp.full(row.shape, magnify_ref[first], jnp.float32)
        for i in range(1, GROUP):
            lane_factor = jnp.where(lane_id >= i * slab_rows, magnify_ref[first + i], lane_factor)
        row_table[group] = jnp.maximum(
            0.0, 1.0 - jnp.abs(detector / lane_factor - axial)
        ).astype(jnp.bfloat16)

        for i in range(GROUP):
            rate = 1.0 / magnify_ref[first + i]
            starts = run_starts((0.5 - half) * rate + (half - 0.75), RUN * rate, cols - LANES)
            out_rows = slice(i * slab_rows, (i + 1) * slab_rows)
            if i % FETCHED == 0:
                fetch(group * (GROUP // FETCHED) + i // FETCHED).wait()
            before = None
            for g in range(blocks + 1):
                here = slice(g * LANES, (g + 1) * LANES)
                values = window(next(starts), volume, (first + i, slice(None)))
                lanes = jnp.broadcast_to(source[i : i + 1, here], values.shape).astype(jnp.int16)
                run = interpolated(
                    values, lanes, (low[i : i + 1, here], high[i : i + 1, here])
                )
                if before is not None:
                    resampled[group, out_rows, (g - 1) * LANES : g * LANES] = joined(
                        g - 1, before, run
                    )
                before = run
        return carry

    lax.fori_loop(0, groups, group_step, 0)

    upward = lax.axis_index("row") % 2 == 0
    r = slab_rows
    for c in range(0, cols, 512):
        here = slice(c, c + 512)
        frame = None
        for group in range(groups):
            part = jnp.dot(
                row_table[group], resampled[group, :, here], preferred_element_type=jnp.float32
            )
            frame = part if frame is None else frame + part
        own_ref[:, here] = frame[2 * r : 3 * r]
        near_ref[:, here] = jnp.where(upward, frame[3 * r : 4 * r], frame[r : 2 * r])
        far_ref[:, here] = jnp.where(upward, frame[4 * r :], frame[:r])
        send_ref[:r, here] = jnp.where(upward, frame[r : 2 * r], frame[3 * r : 4 * r]).astype(
            send_ref.dtype
        )
        send_ref[r:, here] = jnp.where(upward, frame[:r], frame[4 * r :]).astype(send_ref.dtype)


def backward_kernel(
    magnify_ref, own_ref, halo_ref, out_ref,
    out, departure, frame, row_table, smeared, source, weight0, weight1, weight2,
):
    planes, slab_rows, cols = out_ref.shape
    groups = planes // GROUP
    half = cols // 2
    blocks = cols // LANES
    vol_first = lax.axis_index("slab") * slab_rows
    middle = slab_rows * lax.axis_size("slab") // 2

    def store(part):
        planes_of = pl.ds(part * SENT, SENT)
        return pltpu.make_async_copy(out.at[planes_of], out_ref.at[planes_of], departure.at[part])

    r = slab_rows
    frame[:r, :] = halo_ref[0, r:, :]
    frame[r : 2 * r, :] = halo_ref[0, :r, :]
    frame[2 * r : 3 * r, :] = own_ref[...]
    frame[3 * r : 5 * r, :] = halo_ref[1]
    frame[5 * r :, :] = jnp.zeros((frame.shape[0] - 5 * r, cols), frame.dtype)

    row = lax.broadcasted_iota(jnp.int32, (slab_rows, LANES), 0)
    lane_id = lax.broadcasted_iota(jnp.int32, (slab_rows, LANES), 1)
    axial = (row + vol_first).astype(jnp.float32) - (middle - 0.5)
    detector = (lane_id + (vol_first - REACH * slab_rows)).astype(jnp.float32) + (0.5 - middle)
    for i in range(planes):
        row_table[i * r : (i + 1) * r, :] = jnp.maximum(
            0.0, 1.0 - jnp.abs(detector / magnify_ref[i] - axial)
        ).astype(jnp.bfloat16)
    for c in range(0, cols, 256):
        smeared[:, c : c + 256] = jnp.dot(
            row_table[...], frame[:, c : c + 256], preferred_element_type=jnp.float32
        ).astype(jnp.bfloat16)

    lane = lax.broadcasted_iota(jnp.int32, (GROUP, LANES), 1)

    def group_step(group, carry):
        first = group * GROUP
        factors = factors_on_sublanes(magnify_ref, first)
        for g in range(blocks + 1):
            target = run_columns(g, lane).astype(jnp.float32)
            tap = jnp.floor((target - (half + 0.5)) * factors + (half - 0.501)) + 1.0
            here = slice(g * LANES, (g + 1) * LANES)
            source[:, here] = tap.astype(jnp.int32) & (LANES - 1)
            for step, weight in enumerate((weight0, weight1, weight2)):
                column = tap + step
                at = (column + (0.5 - half)) / factors + (half - 0.5)
                weight[:, here] = jnp.where(
                    (column >= 0.0) & (column < cols),
                    rounded(jnp.maximum(0.0, 1.0 - jnp.abs(at - target))),
                    0.0,
                )

        for i in range(GROUP):
            factor = magnify_ref[first + i]
            starts = run_starts(
                (-half - 0.5) * factor + (half + 0.249), RUN * factor, cols - LANES
            )
            rows = (pl.ds(pl.multiple_of((first + i) * r, r), r),)
            before = None
            for g in range(blocks + 1):
                here = slice(g * LANES, (g + 1) * LANES)
                values = window(next(starts), smeared, rows)
                lanes = jnp.broadcast_to(source[i : i + 1, here], values.shape).astype(jnp.int16)
                run = interpolated(
                    values, lanes, [w[i : i + 1, here] for w in (weight0, weight1, weight2)]
                )
                if before is not None:
                    out[first + i, :, (g - 1) * LANES : g * LANES] = joined(g - 1, before, run)
                before = run
            if (i + 1) % SENT == 0:
                store(group * (GROUP // SENT) + i // SENT).start()
        return carry

    lax.fori_loop(0, groups, group_step, 0)
    for part in range(planes // SENT):
        store(part).wait()


PARAMS = pltpu.CompilerParams(vmem_limit_bytes=53 << 20)
SMEM = pl.BlockSpec(memory_space=pltpu.SMEM)
VMEM = pl.BlockSpec(memory_space=pltpu.VMEM)
ANY = pl.BlockSpec(memory_space=pl.ANY)


def forward(magnify, volume):
    planes, slab_rows, cols = volume.shape
    groups = planes // GROUP
    band = (slab_rows, cols)
    pair = (2 * slab_rows, cols)
    run_cols = cols + LANES
    return pl.pallas_call(
        forward_kernel,
        in_specs=[SMEM, ANY],
        out_specs=[VMEM] * 4,
        out_shape=[jax.ShapeDtypeStruct(band, jnp.float32)] * 3
        + [jax.ShapeDtypeStruct(pair, jnp.bfloat16)],
        scratch_shapes=[
            pltpu.VMEM((planes, slab_rows, run_cols), volume.dtype),
            pltpu.SemaphoreType.DMA((planes // FETCHED,)),
            pltpu.VMEM((groups, GROUP * slab_rows, cols), jnp.bfloat16),
            pltpu.VMEM((groups, BLOCKS * slab_rows, GROUP * slab_rows), jnp.bfloat16),
            pltpu.VMEM((GROUP, run_cols), jnp.int32),
            pltpu.VMEM((GROUP, run_cols), jnp.float32),
            pltpu.VMEM((GROUP, run_cols), jnp.float32),
        ],
        compiler_params=PARAMS,
        name="forward_planes",
    )(magnify, volume)


def backward(magnify, residual, halo):
    planes = magnify.shape[0]
    slab_rows, cols = residual.shape
    run_cols = cols + LANES
    shape = (planes, slab_rows, cols)
    return pl.pallas_call(
        backward_kernel,
        in_specs=[SMEM, VMEM, VMEM],
        out_specs=ANY,
        out_shape=jax.ShapeDtypeStruct(shape, jnp.bfloat16),
        scratch_shapes=[
            pltpu.VMEM(shape, jnp.bfloat16),
            pltpu.SemaphoreType.DMA((planes // SENT,)),
            pltpu.VMEM((LANES, cols), jnp.bfloat16),
            pltpu.VMEM((planes * slab_rows, LANES), jnp.bfloat16),
            pltpu.VMEM((planes * slab_rows, run_cols), jnp.bfloat16),
            pltpu.VMEM((GROUP, run_cols), jnp.int32),
            pltpu.VMEM((GROUP, run_cols), jnp.float32),
            pltpu.VMEM((GROUP, run_cols), jnp.float32),
            pltpu.VMEM((GROUP, run_cols), jnp.float32),
        ],
        compiler_params=PARAMS,
        name="backward_planes",
    )(magnify, residual, halo)


def both_ways(block, distance):
    slabs, members = lax.axis_size("slab"), lax.axis_size("row")
    route = []
    for s in range(slabs):
        for q in range(members):
            to = s + (distance if q % 2 == 0 else -distance)
            if 0 <= to < slabs:
                crosses = distance == 1 and s // CHIP_RUN != to // CHIP_RUN
                route.append((s * members + q, to * members + (q ^ 2 if crosses else q)))
    return lax.ppermute(block, ("slab", "row"), route)


def shards(volume, magnify, goal, live_pixels):
    slab_rows, own_cols = goal.shape
    row_count = lax.axis_size("row")
    cols = own_cols * row_count

    pairs = [[q, q + 1] for q in range(0, row_count, 2)]
    own, near, far, send = forward(magnify, volume)
    got = lax.ppermute(send, "row", [(q, q ^ 1) for q in range(row_count)]).astype(jnp.float32)
    near = both_ways((near + got[:slab_rows]).astype(jnp.bfloat16), 1)
    far = both_ways((far + got[slab_rows:]).astype(jnp.bfloat16), 2)
    total = own + near.astype(jnp.float32) + far.astype(jnp.float32)

    coarse = goal.astype(jnp.bfloat16)
    fine = (goal - coarse.astype(jnp.float32)).astype(jnp.bfloat16)
    coarse = jnp.where(live_pixels == 0, jnp.bfloat16(DEAD), coarse)
    message = jnp.concatenate([total.astype(jnp.bfloat16), coarse, fine], axis=1)
    other = lax.ppermute(message, "row", [(q, q ^ 2) for q in range(row_count)])
    total = total + other[:, :cols].astype(jnp.float32)
    message = jnp.concatenate([total.astype(jnp.bfloat16), message[:, cols:], other[:, cols:]], axis=1)
    gathered = lax.all_gather(message, "row", axis_index_groups=pairs).astype(jnp.float32)
    projection = gathered[:, :, :cols].sum(axis=0)
    lower_half = lax.axis_index("row") < 2
    mine, others = gathered[:, :, cols : cols + 2 * own_cols], gathered[:, :, cols + 2 * own_cols :]
    members = [jnp.where(lower_half, mine, others), jnp.where(lower_half, others, mine)]
    members = [half[core] for half in members for core in range(2)]
    all_coarse = jnp.concatenate([goals[:, :own_cols] for goals in members], axis=1)
    all_fine = jnp.concatenate([goals[:, own_cols:] for goals in members], axis=1)
    residual = jnp.where(
        all_coarse > 0.5 * DEAD, 0.0, projection - (all_coarse + all_fine)
    ).astype(jnp.bfloat16)
    own_projection = lax.dynamic_slice_in_dim(
        projection, lax.axis_index("row") * own_cols, own_cols, axis=1
    )

    arrived = jnp.concatenate([both_ways(residual, 1), both_ways(residual, 2)], axis=0)
    halo = lax.all_gather(arrived, "row", axis_index_groups=pairs)
    return (own_projection, backward(magnify, residual, halo))


def solution(mesh):
    in_specs = (P("row", "slab", None), P("row"), P("slab", "row"), P("slab", "row"))
    out_specs = (P("slab", "row"), P("row", "slab", None))
    return jax.shard_map(shards, mesh=mesh, in_specs=in_specs, out_specs=out_specs, check_vma=False)
```

```python
import jax
import jax.numpy as jnp
from jax import lax
from jax.experimental import pallas as pl
from jax.experimental.pallas import tpu as pltpu
from jax.sharding import PartitionSpec as P

REACH = 2
BLOCKS = 2 * REACH + 1
LANES = 128
LANE_BITS = 7
FIXED_BITS = 16
FIXED = float(1 << FIXED_BITS)
GROUP = 8
SENT = 4
FETCHED = 8
RUN = 121
DEAD = 1e30

LANE_GATHER = lax.GatherDimensionNumbers(
    offset_dims=(),
    collapsed_slice_dims=(1,),
    start_index_map=(1,),
    operand_batching_dims=(0,),
    start_indices_batching_dims=(0,),
)


def pick(block, lanes):
    return lax.gather(
        block,
        lanes[..., None],
        LANE_GATHER,
        (1, 1),
        mode=lax.GatherScatterMode.PROMISE_IN_BOUNDS,
    )


def window(start, ref, rows):
    block = pl.multiple_of((start >> LANE_BITS) * LANES, LANES)
    one = ref[rows + (pl.ds(block, LANES),)]
    two = ref[rows + (pl.ds(block + LANES, LANES),)]
    lane = lax.broadcasted_iota(jnp.int32, one.shape, 1).astype(jnp.int16)
    edge = jnp.full(one.shape, start & (LANES - 1), jnp.int32).astype(jnp.int16)
    return jnp.where(lane >= edge, one, two)


def joined(group, before, after):
    lane = lax.broadcasted_iota(jnp.int32, before.shape, 1).astype(jnp.int16)
    return jnp.where(lane < RUN - (LANES - RUN) * group, before, after)


def run_columns(group, lane):
    return lane + jnp.where(lane >= LANES - (LANES - RUN) * group, group - 1, group) * LANES


def run_starts(first, stride, last):
    at = (first * FIXED).astype(jnp.int32)
    step = (stride * FIXED).astype(jnp.int32)
    while True:
        yield jnp.clip(at >> FIXED_BITS, 0, last)
        at = at + step


def factors_on_sublanes(magnify_ref, first):
    plane = lax.broadcasted_iota(jnp.int32, (GROUP, LANES), 0)
    factors = jnp.full((GROUP, LANES), magnify_ref[first], jnp.float32)
    for i in range(1, GROUP):
        factors = jnp.where(plane == i, magnify_ref[first + i], factors)
    return factors


def rounded(weights):
    return weights.astype(jnp.bfloat16).astype(jnp.float32)


def interpolated(values, lanes, weights):
    total = None
    for step, weight in enumerate(weights):
        picked = pick(values, (lanes + step) & (LANES - 1) if step else lanes)
        term = picked.astype(jnp.float32) * weight
        total = term if total is None else total + term
    return total.astype(values.dtype)


def forward_kernel(
    magnify_ref, volume_ref, own_ref, near_ref, far_ref, send_ref,
    volume, arrival, resampled, row_table, source, low, high,
):
    planes, slab_rows, cols = volume_ref.shape
    groups = planes // GROUP
    half = cols // 2
    blocks = cols // LANES
    frame_rows = BLOCKS * slab_rows
    vol_first = lax.axis_index("slab") * slab_rows
    middle = slab_rows * lax.axis_size("slab") // 2

    def fetch(part):
        planes_of = pl.ds(part * FETCHED, FETCHED)
        return pltpu.make_async_copy(
            volume_ref.at[planes_of], volume.at[planes_of, :, pl.ds(0, cols)], arrival.at[part]
        )

    for part in range(planes // FETCHED):
        fetch(part).start()

    lane = lax.broadcasted_iota(jnp.int32, (GROUP, LANES), 1)
    row = lax.broadcasted_iota(jnp.int32, (frame_rows, GROUP * slab_rows), 0)
    lane_id = lax.broadcasted_iota(jnp.int32, (frame_rows, GROUP * slab_rows), 1)
    detector = (row + (vol_first - REACH * slab_rows)).astype(jnp.float32) + (0.5 - middle)
    axial = ((lane_id & (slab_rows - 1)) + vol_first).astype(jnp.float32) - (middle - 0.5)

    def group_step(group, carry):
        first = group * GROUP
        factors = factors_on_sublanes(magnify_ref, first)
        for g in range(blocks + 1):
            column = run_columns(g, lane).astype(jnp.float32)
            at = (column + 0.5 - half) / factors + (half - 0.5)
            floor_at = jnp.floor(at)
            part = at - floor_at
            position = floor_at.astype(jnp.int32)
            here = slice(g * LANES, (g + 1) * LANES)
            source[:, here] = position & (LANES - 1)
            low[:, here] = jnp.where(
                (position >= 0) & (position < cols), rounded(1.0 - part), 0.0
            )
            high[:, here] = jnp.where(
                (position >= -1) & (position < cols - 1), rounded(part), 0.0
            )

        lane_factor = jnp.full(row.shape, magnify_ref[first], jnp.float32)
        for i in range(1, GROUP):
            lane_factor = jnp.where(lane_id >= i * slab_rows, magnify_ref[first + i], lane_factor)
        row_table[group] = jnp.maximum(
            0.0, 1.0 - jnp.abs(detector / lane_factor - axial)
        ).astype(jnp.bfloat16)

        for i in range(GROUP):
            rate = 1.0 / magnify_ref[first + i]
            starts = run_starts((0.5 - half) * rate + (half - 0.75), RUN * rate, cols - LANES)
            out_rows = slice(i * slab_rows, (i + 1) * slab_rows)
            if i % FETCHED == 0:
                fetch(group * (GROUP // FETCHED) + i // FETCHED).wait()
            before = None
            for g in range(blocks + 1):
                here = slice(g * LANES, (g + 1) * LANES)
                values = window(next(starts), volume, (first + i, slice(None)))
                lanes = jnp.broadcast_to(source[i : i + 1, here], values.shape).astype(jnp.int16)
                run = interpolated(
                    values, lanes, (low[i : i + 1, here], high[i : i + 1, here])
                )
                if before is not None:
                    resampled[group, out_rows, (g - 1) * LANES : g * LANES] = joined(
                        g - 1, before, run
                    )
                before = run
        return carry

    lax.fori_loop(0, groups, group_step, 0)

    upward = lax.axis_index("row") % 2 == 0
    r = slab_rows
    for c in range(0, cols, 512):
        here = slice(c, c + 512)
        frame = None
        for group in range(groups):
            part = jnp.dot(
                row_table[group], resampled[group, :, here], preferred_element_type=jnp.float32
            )
            frame = part if frame is None else frame + part
        own_ref[:, here] = frame[2 * r : 3 * r]
        near_ref[:, here] = jnp.where(upward, frame[3 * r : 4 * r], frame[r : 2 * r])
        far_ref[:, here] = jnp.where(upward, frame[4 * r :], frame[:r])
        send_ref[:r, here] = jnp.where(upward, frame[r : 2 * r], frame[3 * r : 4 * r]).astype(
            send_ref.dtype
        )
        send_ref[r:, here] = jnp.where(upward, frame[:r], frame[4 * r :]).astype(send_ref.dtype)


def backward_kernel(
    magnify_ref, own_ref, halo_ref, out_ref,
    out, departure, frame, row_table, smeared, source, weight0, weight1, weight2,
):
    planes, slab_rows, cols = out_ref.shape
    groups = planes // GROUP
    half = cols // 2
    blocks = cols // LANES
    vol_first = lax.axis_index("slab") * slab_rows
    middle = slab_rows * lax.axis_size("slab") // 2

    def store(part):
        planes_of = pl.ds(part * SENT, SENT)
        return pltpu.make_async_copy(out.at[planes_of], out_ref.at[planes_of], departure.at[part])

    r = slab_rows
    frame[:r, :] = halo_ref[0, r:, :]
    frame[r : 2 * r, :] = halo_ref[0, :r, :]
    frame[2 * r : 3 * r, :] = own_ref[...]
    frame[3 * r : 5 * r, :] = halo_ref[1]
    frame[5 * r :, :] = jnp.zeros((frame.shape[0] - 5 * r, cols), frame.dtype)

    row = lax.broadcasted_iota(jnp.int32, (slab_rows, LANES), 0)
    lane_id = lax.broadcasted_iota(jnp.int32, (slab_rows, LANES), 1)
    axial = (row + vol_first).astype(jnp.float32) - (middle - 0.5)
    detector = (lane_id + (vol_first - REACH * slab_rows)).astype(jnp.float32) + (0.5 - middle)
    for i in range(planes):
        row_table[i * r : (i + 1) * r, :] = jnp.maximum(
            0.0, 1.0 - jnp.abs(detector / magnify_ref[i] - axial)
        ).astype(jnp.bfloat16)
    for c in range(0, cols, 256):
        smeared[:, c : c + 256] = jnp.dot(
            row_table[...], frame[:, c : c + 256], preferred_element_type=jnp.float32
        ).astype(jnp.bfloat16)

    lane = lax.broadcasted_iota(jnp.int32, (GROUP, LANES), 1)

    def group_step(group, carry):
        first = group * GROUP
        factors = factors_on_sublanes(magnify_ref, first)
        for g in range(blocks + 1):
            target = run_columns(g, lane).astype(jnp.float32)
            tap = jnp.floor((target - (half + 0.5)) * factors + (half - 0.501)) + 1.0
            here = slice(g * LANES, (g + 1) * LANES)
            source[:, here] = tap.astype(jnp.int32) & (LANES - 1)
            for step, weight in enumerate((weight0, weight1, weight2)):
                column = tap + step
                at = (column + (0.5 - half)) / factors + (half - 0.5)
                weight[:, here] = jnp.where(
                    (column >= 0.0) & (column < cols),
                    rounded(jnp.maximum(0.0, 1.0 - jnp.abs(at - target))),
                    0.0,
                )

        for i in range(GROUP):
            factor = magnify_ref[first + i]
            starts = run_starts(
                (-half - 0.5) * factor + (half + 0.249), RUN * factor, cols - LANES
            )
            rows = (pl.ds(pl.multiple_of((first + i) * r, r), r),)
            before = None
            for g in range(blocks + 1):
                here = slice(g * LANES, (g + 1) * LANES)
                values = window(next(starts), smeared, rows)
                lanes = jnp.broadcast_to(source[i : i + 1, here], values.shape).astype(jnp.int16)
                run = interpolated(
                    values, lanes, [w[i : i + 1, here] for w in (weight0, weight1, weight2)]
                )
                if before is not None:
                    out[first + i, :, (g - 1) * LANES : g * LANES] = joined(g - 1, before, run)
                before = run
            if (i + 1) % SENT == 0:
                store(group * (GROUP // SENT) + i // SENT).start()
        return carry

    lax.fori_loop(0, groups, group_step, 0)
    for part in range(planes // SENT):
        store(part).wait()


PARAMS = pltpu.CompilerParams(vmem_limit_bytes=53 << 20)
SMEM = pl.BlockSpec(memory_space=pltpu.SMEM)
VMEM = pl.BlockSpec(memory_space=pltpu.VMEM)
ANY = pl.BlockSpec(memory_space=pl.ANY)


def forward(magnify, volume):
    planes, slab_rows, cols = volume.shape
    groups = planes // GROUP
    band = (slab_rows, cols)
    pair = (2 * slab_rows, cols)
    run_cols = cols + LANES
    return pl.pallas_call(
        forward_kernel,
        in_specs=[SMEM, ANY],
        out_specs=[VMEM] * 4,
        out_shape=[jax.ShapeDtypeStruct(band, jnp.float32)] * 3
        + [jax.ShapeDtypeStruct(pair, jnp.bfloat16)],
        scratch_shapes=[
            pltpu.VMEM((planes, slab_rows, run_cols), volume.dtype),
            pltpu.SemaphoreType.DMA((planes // FETCHED,)),
            pltpu.VMEM((groups, GROUP * slab_rows, cols), jnp.bfloat16),
            pltpu.VMEM((groups, BLOCKS * slab_rows, GROUP * slab_rows), jnp.bfloat16),
            pltpu.VMEM((GROUP, run_cols), jnp.int32),
            pltpu.VMEM((GROUP, run_cols), jnp.float32),
            pltpu.VMEM((GROUP, run_cols), jnp.float32),
        ],
        compiler_params=PARAMS,
        name="forward_planes",
    )(magnify, volume)


def backward(magnify, residual, halo):
    planes = magnify.shape[0]
    slab_rows, cols = residual.shape
    run_cols = cols + LANES
    shape = (planes, slab_rows, cols)
    return pl.pallas_call(
        backward_kernel,
        in_specs=[SMEM, VMEM, VMEM],
        out_specs=ANY,
        out_shape=jax.ShapeDtypeStruct(shape, jnp.bfloat16),
        scratch_shapes=[
            pltpu.VMEM(shape, jnp.bfloat16),
            pltpu.SemaphoreType.DMA((planes // SENT,)),
            pltpu.VMEM((LANES, cols), jnp.bfloat16),
            pltpu.VMEM((planes * slab_rows, LANES), jnp.bfloat16),
            pltpu.VMEM((planes * slab_rows, run_cols), jnp.bfloat16),
            pltpu.VMEM((GROUP, run_cols), jnp.int32),
            pltpu.VMEM((GROUP, run_cols), jnp.float32),
            pltpu.VMEM((GROUP, run_cols), jnp.float32),
            pltpu.VMEM((GROUP, run_cols), jnp.float32),
        ],
        compiler_params=PARAMS,
        name="backward_planes",
    )(magnify, residual, halo)


def reaches(slab, other, slab_rows, rows_all):
    half = rows_all / 2
    spread = (REACH * slab_rows - 3.0) / (half + 1.0)
    least, most = slab * slab_rows - 1.1, (slab + 1) * slab_rows + 0.1
    for detector in range(other * slab_rows, (other + 1) * slab_rows):
        from_middle = detector + 0.5 - half
        ends = (from_middle / (1.0 - spread), from_middle / (1.0 + spread))
        if max(ends) + half - 0.5 > least and min(ends) + half - 0.5 < most:
            return True
    return False


def both_ways(block, distance, samples):
    slab_rows = block.shape[0]
    slabs, members = lax.axis_size("slab"), lax.axis_size("row")
    route = []
    for s in range(slabs):
        for q in range(members):
            to = s + (distance if q % 2 == 0 else -distance)
            if 0 <= to < slabs:
                rows_of, block_of = (s, to) if samples else (to, s)
                if reaches(rows_of, block_of, slab_rows, slab_rows * slabs):
                    route.append((s * members + q, to * members + q))
    return lax.ppermute(block, ("slab", "row"), route)


def shards(volume, magnify, goal, live_pixels):
    slab_rows, own_cols = goal.shape
    row_count = lax.axis_size("row")
    cols = own_cols * row_count

    pairs = [[q, q + 1] for q in range(0, row_count, 2)]
    own, near, far, send = forward(magnify, volume)
    got = lax.ppermute(send, "row", [(q, q ^ 1) for q in range(row_count)]).astype(jnp.float32)
    near = both_ways((near + got[:slab_rows]).astype(jnp.bfloat16), 1, True)
    far = both_ways((far + got[slab_rows:]).astype(jnp.bfloat16), 2, True)
    total = own + near.astype(jnp.float32) + far.astype(jnp.float32)

    coarse = goal.astype(jnp.bfloat16)
    fine = (goal - coarse.astype(jnp.float32)).astype(jnp.bfloat16)
    coarse = jnp.where(live_pixels == 0, jnp.bfloat16(DEAD), coarse)
    message = jnp.concatenate([total.astype(jnp.bfloat16), coarse, fine], axis=1)
    other = lax.ppermute(message, "row", [(q, q ^ 2) for q in range(row_count)])
    total = total + other[:, :cols].astype(jnp.float32)
    message = jnp.concatenate([total.astype(jnp.bfloat16), message[:, cols:], other[:, cols:]], axis=1)
    gathered = lax.all_gather(message, "row", axis_index_groups=pairs).astype(jnp.float32)
    projection = gathered[:, :, :cols].sum(axis=0)
    lower_half = lax.axis_index("row") < 2
    mine, others = gathered[:, :, cols : cols + 2 * own_cols], gathered[:, :, cols + 2 * own_cols :]
    members = [jnp.where(lower_half, mine, others), jnp.where(lower_half, others, mine)]
    members = [half[core] for half in members for core in range(2)]
    all_coarse = jnp.concatenate([goals[:, :own_cols] for goals in members], axis=1)
    all_fine = jnp.concatenate([goals[:, own_cols:] for goals in members], axis=1)
    residual = jnp.where(
        all_coarse > 0.5 * DEAD, 0.0, projection - (all_coarse + all_fine)
    ).astype(jnp.bfloat16)
    own_projection = lax.dynamic_slice_in_dim(
        projection, lax.axis_index("row") * own_cols, own_cols, axis=1
    )

    arrived = jnp.concatenate([both_ways(residual, 1, False), both_ways(residual, 2, False)], axis=0)
    halo = lax.all_gather(arrived, "row", axis_index_groups=pairs)
    return (own_projection, backward(magnify, residual, halo))


def solution(mesh):
    in_specs = (P("row", "slab", None), P("row"), P("slab", "row"), P("slab", "row"))
    out_specs = (P("slab", "row"), P("row", "slab", None))
    return jax.shard_map(shards, mesh=mesh, in_specs=in_specs, out_specs=out_specs, check_vma=False)
```

```python
import jax
import jax.numpy as jnp
from jax import lax
from jax.experimental import pallas as pl
from jax.experimental.pallas import tpu as pltpu
from jax.sharding import PartitionSpec as P

REACH = 2
BLOCKS = 2 * REACH + 1
LANES = 128
LANE_BITS = 7
FIXED_BITS = 16
FIXED = float(1 << FIXED_BITS)
GROUP = 8
SENT = 4
FETCHED = 8
RUN = 121
DEAD = 1e30

LANE_GATHER = lax.GatherDimensionNumbers(
    offset_dims=(),
    collapsed_slice_dims=(1,),
    start_index_map=(1,),
    operand_batching_dims=(0,),
    start_indices_batching_dims=(0,),
)


def pick(block, lanes):
    return lax.gather(
        block,
        lanes[..., None],
        LANE_GATHER,
        (1, 1),
        mode=lax.GatherScatterMode.PROMISE_IN_BOUNDS,
    )


def window(start, ref, rows):
    block = pl.multiple_of((start >> LANE_BITS) * LANES, LANES)
    one = ref[rows + (pl.ds(block, LANES),)]
    two = ref[rows + (pl.ds(block + LANES, LANES),)]
    lane = lax.broadcasted_iota(jnp.int32, one.shape, 1).astype(jnp.int16)
    edge = jnp.full(one.shape, start & (LANES - 1), jnp.int32).astype(jnp.int16)
    return jnp.where(lane >= edge, one, two)


def joined(group, before, after):
    lane = lax.broadcasted_iota(jnp.int32, before.shape, 1).astype(jnp.int16)
    return jnp.where(lane < RUN - (LANES - RUN) * group, before, after)


def run_columns(group, lane):
    return lane + jnp.where(lane >= LANES - (LANES - RUN) * group, group - 1, group) * LANES


def run_starts(first, stride, last):
    at = (first * FIXED).astype(jnp.int32)
    step = (stride * FIXED).astype(jnp.int32)
    while True:
        yield jnp.clip(at >> FIXED_BITS, 0, last)
        at = at + step


def factors_on_sublanes(magnify_ref, first):
    plane = lax.broadcasted_iota(jnp.int32, (GROUP, LANES), 0)
    factors = jnp.full((GROUP, LANES), magnify_ref[first], jnp.float32)
    for i in range(1, GROUP):
        factors = jnp.where(plane == i, magnify_ref[first + i], factors)
    return factors


def rounded(weights):
    return weights.astype(jnp.bfloat16).astype(jnp.float32)


def interpolated(values, lanes, weights):
    total = None
    for step, weight in enumerate(weights):
        picked = pick(values, (lanes + step) & (LANES - 1) if step else lanes)
        term = picked.astype(jnp.float32) * weight
        total = term if total is None else total + term
    return total.astype(values.dtype)


def forward_kernel(
    magnify_in, volume_ref, own_ref, near_ref, far_ref, send_ref,
    magnify_ref, noted, volume, arrival, resampled, row_table, source, low, high,
):
    planes, slab_rows, cols = volume_ref.shape
    groups = planes // GROUP
    half = cols // 2
    blocks = cols // LANES
    frame_rows = BLOCKS * slab_rows
    vol_first = lax.axis_index("slab") * slab_rows
    middle = slab_rows * lax.axis_size("slab") // 2

    def fetch(part):
        planes_of = pl.ds(part * FETCHED, FETCHED)
        return pltpu.make_async_copy(
            volume_ref.at[planes_of], volume.at[planes_of, :, pl.ds(0, cols)], arrival.at[part]
        )

    note = pltpu.make_async_copy(magnify_in, magnify_ref, noted)
    note.start()
    for part in range(planes // FETCHED):
        fetch(part).start()
    note.wait()

    lane = lax.broadcasted_iota(jnp.int32, (GROUP, LANES), 1)
    row = lax.broadcasted_iota(jnp.int32, (frame_rows, GROUP * slab_rows), 0)
    lane_id = lax.broadcasted_iota(jnp.int32, (frame_rows, GROUP * slab_rows), 1)
    detector = (row + (vol_first - REACH * slab_rows)).astype(jnp.float32) + (0.5 - middle)
    axial = ((lane_id & (slab_rows - 1)) + vol_first).astype(jnp.float32) - (middle - 0.5)

    def group_step(group, carry):
        first = group * GROUP
        factors = factors_on_sublanes(magnify_ref, first)
        for g in range(blocks + 1):
            column = run_columns(g, lane).astype(jnp.float32)
            at = (column + 0.5 - half) / factors + (half - 0.5)
            floor_at = jnp.floor(at)
            part = at - floor_at
            position = floor_at.astype(jnp.int32)
            here = slice(g * LANES, (g + 1) * LANES)
            source[:, here] = position & (LANES - 1)
            low[:, here] = jnp.where(
                (position >= 0) & (position < cols), rounded(1.0 - part), 0.0
            )
            high[:, here] = jnp.where(
                (position >= -1) & (position < cols - 1), rounded(part), 0.0
            )

        lane_factor = jnp.full(row.shape, magnify_ref[first], jnp.float32)
        for i in range(1, GROUP):
            lane_factor = jnp.where(lane_id >= i * slab_rows, magnify_ref[first + i], lane_factor)
        row_table[group] = jnp.maximum(
            0.0, 1.0 - jnp.abs(detector / lane_factor - axial)
        ).astype(jnp.bfloat16)

        for i in range(GROUP):
            rate = 1.0 / magnify_ref[first + i]
            starts = run_starts((0.5 - half) * rate + (half - 0.75), RUN * rate, cols - LANES)
            out_rows = slice(i * slab_rows, (i + 1) * slab_rows)
            if i % FETCHED == 0:
                fetch(group * (GROUP // FETCHED) + i // FETCHED).wait()
            before = None
            for g in range(blocks + 1):
                here = slice(g * LANES, (g + 1) * LANES)
                values = window(next(starts), volume, (first + i, slice(None)))
                lanes = jnp.broadcast_to(source[i : i + 1, here], values.shape).astype(jnp.int16)
                run = interpolated(
                    values, lanes, (low[i : i + 1, here], high[i : i + 1, here])
                )
                if before is not None:
                    resampled[group, out_rows, (g - 1) * LANES : g * LANES] = joined(
                        g - 1, before, run
                    )
                before = run
        return carry

    lax.fori_loop(0, groups, group_step, 0)

    upward = lax.axis_index("row") % 2 == 0
    r = slab_rows
    for c in range(0, cols, 512):
        here = slice(c, c + 512)
        frame = None
        for group in range(groups):
            part = jnp.dot(
                row_table[group], resampled[group, :, here], preferred_element_type=jnp.float32
            )
            frame = part if frame is None else frame + part
        own_ref[:, here] = frame[2 * r : 3 * r]
        near_ref[:, here] = jnp.where(upward, frame[3 * r : 4 * r], frame[r : 2 * r])
        far_ref[:, here] = jnp.where(upward, frame[4 * r :], frame[:r])
        send_ref[:r, here] = jnp.where(upward, frame[r : 2 * r], frame[3 * r : 4 * r]).astype(
            send_ref.dtype
        )
        send_ref[r:, here] = jnp.where(upward, frame[:r], frame[4 * r :]).astype(send_ref.dtype)


def backward_kernel(
    magnify_ref, own_ref, halo_ref, out_ref,
    out, departure, frame, row_table, smeared, source, weight0, weight1, weight2,
):
    planes, slab_rows, cols = out_ref.shape
    groups = planes // GROUP
    half = cols // 2
    blocks = cols // LANES
    vol_first = lax.axis_index("slab") * slab_rows
    middle = slab_rows * lax.axis_size("slab") // 2

    def store(part):
        planes_of = pl.ds(part * SENT, SENT)
        return pltpu.make_async_copy(out.at[planes_of], out_ref.at[planes_of], departure.at[part])

    r = slab_rows
    frame[:r, :] = halo_ref[0, r:, :]
    frame[r : 2 * r, :] = halo_ref[0, :r, :]
    frame[2 * r : 3 * r, :] = own_ref[...]
    frame[3 * r : 5 * r, :] = halo_ref[1]
    frame[5 * r :, :] = jnp.zeros((frame.shape[0] - 5 * r, cols), frame.dtype)

    row = lax.broadcasted_iota(jnp.int32, (slab_rows, LANES), 0)
    lane_id = lax.broadcasted_iota(jnp.int32, (slab_rows, LANES), 1)
    axial = (row + vol_first).astype(jnp.float32) - (middle - 0.5)
    detector = (lane_id + (vol_first - REACH * slab_rows)).astype(jnp.float32) + (0.5 - middle)
    for i in range(planes):
        row_table[i * r : (i + 1) * r, :] = jnp.maximum(
            0.0, 1.0 - jnp.abs(detector / magnify_ref[i] - axial)
        ).astype(jnp.bfloat16)
    for c in range(0, cols, 256):
        smeared[:, c : c + 256] = jnp.dot(
            row_table[...], frame[:, c : c + 256], preferred_element_type=jnp.float32
        ).astype(jnp.bfloat16)

    lane = lax.broadcasted_iota(jnp.int32, (GROUP, LANES), 1)

    def group_step(group, carry):
        first = group * GROUP
        factors = factors_on_sublanes(magnify_ref, first)
        for g in range(blocks + 1):
            target = run_columns(g, lane).astype(jnp.float32)
            tap = jnp.floor((target - (half + 0.5)) * factors + (half - 0.501)) + 1.0
            here = slice(g * LANES, (g + 1) * LANES)
            source[:, here] = tap.astype(jnp.int32) & (LANES - 1)
            for step, weight in enumerate((weight0, weight1, weight2)):
                column = tap + step
                at = (column + (0.5 - half)) / factors + (half - 0.5)
                weight[:, here] = jnp.where(
                    (column >= 0.0) & (column < cols),
                    rounded(jnp.maximum(0.0, 1.0 - jnp.abs(at - target))),
                    0.0,
                )

        for i in range(GROUP):
            factor = magnify_ref[first + i]
            starts = run_starts(
                (-half - 0.5) * factor + (half + 0.249), RUN * factor, cols - LANES
            )
            rows = (pl.ds(pl.multiple_of((first + i) * r, r), r),)
            before = None
            for g in range(blocks + 1):
                here = slice(g * LANES, (g + 1) * LANES)
                values = window(next(starts), smeared, rows)
                lanes = jnp.broadcast_to(source[i : i + 1, here], values.shape).astype(jnp.int16)
                run = interpolated(
                    values, lanes, [w[i : i + 1, here] for w in (weight0, weight1, weight2)]
                )
                if before is not None:
                    out[first + i, :, (g - 1) * LANES : g * LANES] = joined(g - 1, before, run)
                before = run
            if (i + 1) % SENT == 0:
                store(group * (GROUP // SENT) + i // SENT).start()
        return carry

    lax.fori_loop(0, groups, group_step, 0)
    for part in range(planes // SENT):
        store(part).wait()


PARAMS = pltpu.CompilerParams(vmem_limit_bytes=53 << 20)
SMEM = pl.BlockSpec(memory_space=pltpu.SMEM)
VMEM = pl.BlockSpec(memory_space=pltpu.VMEM)
ANY = pl.BlockSpec(memory_space=pl.ANY)


def forward(magnify, volume):
    planes, slab_rows, cols = volume.shape
    groups = planes // GROUP
    band = (slab_rows, cols)
    pair = (2 * slab_rows, cols)
    run_cols = cols + LANES
    return pl.pallas_call(
        forward_kernel,
        in_specs=[ANY, ANY],
        out_specs=[VMEM] * 4,
        out_shape=[jax.ShapeDtypeStruct(band, jnp.float32)] * 3
        + [jax.ShapeDtypeStruct(pair, jnp.bfloat16)],
        scratch_shapes=[
            pltpu.SMEM((planes,), jnp.float32),
            pltpu.SemaphoreType.DMA(()),
            pltpu.VMEM((planes, slab_rows, run_cols), volume.dtype),
            pltpu.SemaphoreType.DMA((planes // FETCHED,)),
            pltpu.VMEM((groups, GROUP * slab_rows, cols), jnp.bfloat16),
            pltpu.VMEM((groups, BLOCKS * slab_rows, GROUP * slab_rows), jnp.bfloat16),
            pltpu.VMEM((GROUP, run_cols), jnp.int32),
            pltpu.VMEM((GROUP, run_cols), jnp.float32),
            pltpu.VMEM((GROUP, run_cols), jnp.float32),
        ],
        compiler_params=PARAMS,
        name="forward_planes",
    )(magnify, volume)


def backward(magnify, residual, halo):
    planes = magnify.shape[0]
    slab_rows, cols = residual.shape
    run_cols = cols + LANES
    shape = (planes, slab_rows, cols)
    return pl.pallas_call(
        backward_kernel,
        in_specs=[SMEM, VMEM, VMEM],
        out_specs=ANY,
        out_shape=jax.ShapeDtypeStruct(shape, jnp.bfloat16),
        scratch_shapes=[
            pltpu.VMEM(shape, jnp.bfloat16),
            pltpu.SemaphoreType.DMA((planes // SENT,)),
            pltpu.VMEM((LANES, cols), jnp.bfloat16),
            pltpu.VMEM((planes * slab_rows, LANES), jnp.bfloat16),
            pltpu.VMEM((planes * slab_rows, run_cols), jnp.bfloat16),
            pltpu.VMEM((GROUP, run_cols), jnp.int32),
            pltpu.VMEM((GROUP, run_cols), jnp.float32),
            pltpu.VMEM((GROUP, run_cols), jnp.float32),
            pltpu.VMEM((GROUP, run_cols), jnp.float32),
        ],
        compiler_params=PARAMS,
        name="backward_planes",
    )(magnify, residual, halo)


def reaches(slab, other, slab_rows, rows_all):
    half = rows_all / 2
    spread = (REACH * slab_rows - 3.0) / (half + 1.0)
    least, most = slab * slab_rows - 1.1, (slab + 1) * slab_rows + 0.1
    for detector in range(other * slab_rows, (other + 1) * slab_rows):
        from_middle = detector + 0.5 - half
        ends = (from_middle / (1.0 - spread), from_middle / (1.0 + spread))
        if max(ends) + half - 0.5 > least and min(ends) + half - 0.5 < most:
            return True
    return False


def both_ways(block, distance, samples):
    slab_rows = block.shape[0]
    slabs, members = lax.axis_size("slab"), lax.axis_size("row")
    route = []
    for s in range(slabs):
        for q in range(members):
            to = s + (distance if q % 2 == 0 else -distance)
            if 0 <= to < slabs:
                rows_of, block_of = (s, to) if samples else (to, s)
                if reaches(rows_of, block_of, slab_rows, slab_rows * slabs):
                    route.append((s * members + q, to * members + q))
    return lax.ppermute(block, ("slab", "row"), route)


def shards(volume, magnify, goal, live_pixels):
    slab_rows, own_cols = goal.shape
    row_count = lax.axis_size("row")
    cols = own_cols * row_count

    pairs = [[q, q + 1] for q in range(0, row_count, 2)]
    across = [[q, q + 2] for q in range(row_count // 2)]
    own, near, far, send = forward(magnify, volume)
    sent = lax.all_gather(send, "row", axis_index_groups=pairs)
    got = jnp.where(lax.axis_index("row") % 2 == 0, sent[1], sent[0]).astype(jnp.float32)
    near = both_ways((near + got[:slab_rows]).astype(jnp.bfloat16), 1, True)
    far = both_ways((far + got[slab_rows:]).astype(jnp.bfloat16), 2, True)
    total = own + near.astype(jnp.float32) + far.astype(jnp.float32)

    coarse = goal.astype(jnp.bfloat16)
    fine = (goal - coarse.astype(jnp.float32)).astype(jnp.bfloat16)
    coarse = jnp.where(live_pixels == 0, jnp.bfloat16(DEAD), coarse)
    message = jnp.concatenate([total.astype(jnp.bfloat16), coarse, fine], axis=1)
    halves = lax.all_gather(message, "row", axis_index_groups=across)
    total = halves[0, :, :cols].astype(jnp.float32) + halves[1, :, :cols].astype(jnp.float32)
    message = jnp.concatenate(
        [total.astype(jnp.bfloat16), halves[0, :, cols:], halves[1, :, cols:]], axis=1
    )
    gathered = lax.all_gather(message, "row", axis_index_groups=pairs).astype(jnp.float32)
    projection = gathered[0, :, :cols] + gathered[1, :, :cols]
    members = [
        gathered[core, :, cols + 2 * half * own_cols : cols + 2 * (half + 1) * own_cols]
        for half in range(2)
        for core in range(2)
    ]
    all_coarse = jnp.concatenate([member[:, :own_cols] for member in members], axis=1)
    all_fine = jnp.concatenate([member[:, own_cols:] for member in members], axis=1)
    residual = jnp.where(
        all_coarse > 0.5 * DEAD, 0.0, projection - (all_coarse + all_fine)
    ).astype(jnp.bfloat16)
    own_projection = lax.dynamic_slice_in_dim(
        projection, lax.axis_index("row") * own_cols, own_cols, axis=1
    )

    arrived = jnp.concatenate([both_ways(residual, 1, False), both_ways(residual, 2, False)], axis=0)
    halo = lax.all_gather(arrived, "row", axis_index_groups=pairs)
    return (own_projection, backward(magnify, residual, halo))


def solution(mesh):
    in_specs = (P("row", "slab", None), P("row"), P("slab", "row"), P("slab", "row"))
    out_specs = (P("slab", "row"), P("row", "slab", None))
    return jax.shard_map(shards, mesh=mesh, in_specs=in_specs, out_specs=out_specs, check_vma=False)
```

```python
import jax
import jax.numpy as jnp
from jax import lax
from jax.experimental import pallas as pl
from jax.experimental.pallas import tpu as pltpu
from jax.sharding import PartitionSpec as P

REACH = 2
BLOCKS = 2 * REACH + 1
LANES = 128
LANE_BITS = 7
FIXED_BITS = 16
FIXED = float(1 << FIXED_BITS)
GROUP = 8
SENT = 4
FETCHED = 8
RUN = 121
DEAD = 1e30

LANE_GATHER = lax.GatherDimensionNumbers(
    offset_dims=(),
    collapsed_slice_dims=(1,),
    start_index_map=(1,),
    operand_batching_dims=(0,),
    start_indices_batching_dims=(0,),
)


def pick(block, lanes):
    return lax.gather(
        block,
        lanes[..., None],
        LANE_GATHER,
        (1, 1),
        mode=lax.GatherScatterMode.PROMISE_IN_BOUNDS,
    )


def window(start, ref, rows):
    block = pl.multiple_of((start >> LANE_BITS) * LANES, LANES)
    one = ref[rows + (pl.ds(block, LANES),)]
    two = ref[rows + (pl.ds(block + LANES, LANES),)]
    lane = lax.broadcasted_iota(jnp.int32, one.shape, 1).astype(jnp.int16)
    edge = jnp.full(one.shape, start & (LANES - 1), jnp.int32).astype(jnp.int16)
    return jnp.where(lane >= edge, one, two)


def joined(group, before, after):
    lane = lax.broadcasted_iota(jnp.int32, before.shape, 1).astype(jnp.int16)
    return jnp.where(lane < RUN - (LANES - RUN) * group, before, after)


def run_columns(group, lane):
    return lane + jnp.where(lane >= LANES - (LANES - RUN) * group, group - 1, group) * LANES


def run_starts(first, stride, last):
    at = (first * FIXED).astype(jnp.int32)
    step = (stride * FIXED).astype(jnp.int32)
    while True:
        yield jnp.clip(at >> FIXED_BITS, 0, last)
        at = at + step


def factors_on_sublanes(magnify_ref, first):
    plane = lax.broadcasted_iota(jnp.int32, (GROUP, LANES), 0)
    factors = jnp.full((GROUP, LANES), magnify_ref[first], jnp.float32)
    for i in range(1, GROUP):
        factors = jnp.where(plane == i, magnify_ref[first + i], factors)
    return factors


def rounded(weights):
    return weights.astype(jnp.bfloat16).astype(jnp.float32)


def interpolated(values, lanes, weights):
    total = None
    for step, weight in enumerate(weights):
        picked = pick(values, (lanes + step) & (LANES - 1) if step else lanes)
        term = picked.astype(jnp.float32) * weight
        total = term if total is None else total + term
    return total.astype(values.dtype)


def forward_kernel(
    magnify_in, volume_ref, own_ref, near_ref, far_ref, send_ref,
    magnify_ref, noted, volume, arrival, resampled, row_table, source, low, high,
):
    planes, slab_rows, cols = volume_ref.shape
    groups = planes // GROUP
    half = cols // 2
    blocks = cols // LANES
    frame_rows = BLOCKS * slab_rows
    vol_first = lax.axis_index("slab") * slab_rows
    middle = slab_rows * lax.axis_size("slab") // 2

    def fetch(part):
        planes_of = pl.ds(part * FETCHED, FETCHED)
        return pltpu.make_async_copy(
            volume_ref.at[planes_of], volume.at[planes_of, :, pl.ds(0, cols)], arrival.at[part]
        )

    note = pltpu.make_async_copy(magnify_in, magnify_ref, noted)
    note.start()
    for part in range(planes // FETCHED):
        fetch(part).start()
    note.wait()

    lane = lax.broadcasted_iota(jnp.int32, (GROUP, LANES), 1)
    row = lax.broadcasted_iota(jnp.int32, (frame_rows, GROUP * slab_rows), 0)
    lane_id = lax.broadcasted_iota(jnp.int32, (frame_rows, GROUP * slab_rows), 1)
    detector = (row + (vol_first - REACH * slab_rows)).astype(jnp.float32) + (0.5 - middle)
    axial = ((lane_id & (slab_rows - 1)) + vol_first).astype(jnp.float32) - (middle - 0.5)

    def group_step(group, carry):
        first = group * GROUP
        factors = factors_on_sublanes(magnify_ref, first)
        for g in range(blocks + 1):
            column = run_columns(g, lane).astype(jnp.float32)
            at = (column + 0.5 - half) / factors + (half - 0.5)
            floor_at = jnp.floor(at)
            part = at - floor_at
            position = floor_at.astype(jnp.int32)
            here = slice(g * LANES, (g + 1) * LANES)
            source[:, here] = position & (LANES - 1)
            low[:, here] = jnp.where(
                (position >= 0) & (position < cols), rounded(1.0 - part), 0.0
            )
            high[:, here] = jnp.where(
                (position >= -1) & (position < cols - 1), rounded(part), 0.0
            )

        lane_factor = jnp.full(row.shape, magnify_ref[first], jnp.float32)
        for i in range(1, GROUP):
            lane_factor = jnp.where(lane_id >= i * slab_rows, magnify_ref[first + i], lane_factor)
        row_table[group] = jnp.maximum(
            0.0, 1.0 - jnp.abs(detector / lane_factor - axial)
        ).astype(jnp.bfloat16)

        for i in range(GROUP):
            rate = 1.0 / magnify_ref[first + i]
            starts = run_starts((0.5 - half) * rate + (half - 0.75), RUN * rate, cols - LANES)
            out_rows = slice(i * slab_rows, (i + 1) * slab_rows)
            if i % FETCHED == 0:
                fetch(group * (GROUP // FETCHED) + i // FETCHED).wait()
            before = None
            for g in range(blocks + 1):
                here = slice(g * LANES, (g + 1) * LANES)
                values = window(next(starts), volume, (first + i, slice(None)))
                lanes = jnp.broadcast_to(source[i : i + 1, here], values.shape).astype(jnp.int16)
                run = interpolated(
                    values, lanes, (low[i : i + 1, here], high[i : i + 1, here])
                )
                if before is not None:
                    resampled[group, out_rows, (g - 1) * LANES : g * LANES] = joined(
                        g - 1, before, run
                    )
                before = run
        return carry

    lax.fori_loop(0, groups, group_step, 0, unroll=True)

    upward = lax.axis_index("row") % 2 == 0
    r = slab_rows
    for c in range(0, cols, 512):
        here = slice(c, c + 512)
        frame = None
        for group in range(groups):
            part = jnp.dot(
                row_table[group], resampled[group, :, here], preferred_element_type=jnp.float32
            )
            frame = part if frame is None else frame + part
        own_ref[:, here] = frame[2 * r : 3 * r]
        near_ref[:, here] = jnp.where(upward, frame[3 * r : 4 * r], frame[r : 2 * r])
        far_ref[:, here] = jnp.where(upward, frame[4 * r :], frame[:r])
        send_ref[:r, here] = jnp.where(upward, frame[r : 2 * r], frame[3 * r : 4 * r]).astype(
            send_ref.dtype
        )
        send_ref[r:, here] = jnp.where(upward, frame[:r], frame[4 * r :]).astype(send_ref.dtype)


def backward_kernel(
    magnify_ref, own_ref, halo_ref, out_ref,
    out, departure, frame, row_table, smeared, source, weight0, weight1, weight2,
):
    planes, slab_rows, cols = out_ref.shape
    groups = planes // GROUP
    half = cols // 2
    blocks = cols // LANES
    vol_first = lax.axis_index("slab") * slab_rows
    middle = slab_rows * lax.axis_size("slab") // 2

    def store(part):
        planes_of = pl.ds(part * SENT, SENT)
        return pltpu.make_async_copy(out.at[planes_of], out_ref.at[planes_of], departure.at[part])

    r = slab_rows
    frame[:r, :] = halo_ref[0, r:, :]
    frame[r : 2 * r, :] = halo_ref[0, :r, :]
    frame[2 * r : 3 * r, :] = own_ref[...]
    frame[3 * r : 5 * r, :] = halo_ref[1]
    frame[5 * r :, :] = jnp.zeros((frame.shape[0] - 5 * r, cols), frame.dtype)

    row = lax.broadcasted_iota(jnp.int32, (slab_rows, LANES), 0)
    lane_id = lax.broadcasted_iota(jnp.int32, (slab_rows, LANES), 1)
    axial = (row + vol_first).astype(jnp.float32) - (middle - 0.5)
    detector = (lane_id + (vol_first - REACH * slab_rows)).astype(jnp.float32) + (0.5 - middle)
    for i in range(planes):
        row_table[i * r : (i + 1) * r, :] = jnp.maximum(
            0.0, 1.0 - jnp.abs(detector / magnify_ref[i] - axial)
        ).astype(jnp.bfloat16)
    for c in range(0, cols, 256):
        smeared[:, c : c + 256] = jnp.dot(
            row_table[...], frame[:, c : c + 256], preferred_element_type=jnp.float32
        ).astype(jnp.bfloat16)

    lane = lax.broadcasted_iota(jnp.int32, (GROUP, LANES), 1)

    def group_step(group, carry):
        first = group * GROUP
        factors = factors_on_sublanes(magnify_ref, first)
        for g in range(blocks + 1):
            target = run_columns(g, lane).astype(jnp.float32)
            tap = jnp.floor((target - (half + 0.5)) * factors + (half - 0.501)) + 1.0
            here = slice(g * LANES, (g + 1) * LANES)
            source[:, here] = tap.astype(jnp.int32) & (LANES - 1)
            for step, weight in enumerate((weight0, weight1, weight2)):
                column = tap + step
                at = (column + (0.5 - half)) / factors + (half - 0.5)
                weight[:, here] = jnp.where(
                    (column >= 0.0) & (column < cols),
                    rounded(jnp.maximum(0.0, 1.0 - jnp.abs(at - target))),
                    0.0,
                )

        for i in range(GROUP):
            factor = magnify_ref[first + i]
            starts = run_starts(
                (-half - 0.5) * factor + (half + 0.249), RUN * factor, cols - LANES
            )
            rows = (pl.ds(pl.multiple_of((first + i) * r, r), r),)
            before = None
            for g in range(blocks + 1):
                here = slice(g * LANES, (g + 1) * LANES)
                values = window(next(starts), smeared, rows)
                lanes = jnp.broadcast_to(source[i : i + 1, here], values.shape).astype(jnp.int16)
                run = interpolated(
                    values, lanes, [w[i : i + 1, here] for w in (weight0, weight1, weight2)]
                )
                if before is not None:
                    out[first + i, :, (g - 1) * LANES : g * LANES] = joined(g - 1, before, run)
                before = run
            if (i + 1) % SENT == 0:
                store(group * (GROUP // SENT) + i // SENT).start()
        return carry

    lax.fori_loop(0, groups, group_step, 0)
    for part in range(planes // SENT):
        store(part).wait()


PARAMS = pltpu.CompilerParams(vmem_limit_bytes=53 << 20)
SMEM = pl.BlockSpec(memory_space=pltpu.SMEM)
VMEM = pl.BlockSpec(memory_space=pltpu.VMEM)
ANY = pl.BlockSpec(memory_space=pl.ANY)


def forward(magnify, volume):
    planes, slab_rows, cols = volume.shape
    groups = planes // GROUP
    band = (slab_rows, cols)
    pair = (2 * slab_rows, cols)
    run_cols = cols + LANES
    return pl.pallas_call(
        forward_kernel,
        in_specs=[ANY, ANY],
        out_specs=[VMEM] * 4,
        out_shape=[jax.ShapeDtypeStruct(band, jnp.float32)] * 3
        + [jax.ShapeDtypeStruct(pair, jnp.bfloat16)],
        scratch_shapes=[
            pltpu.SMEM((planes,), jnp.float32),
            pltpu.SemaphoreType.DMA(()),
            pltpu.VMEM((planes, slab_rows, run_cols), volume.dtype),
            pltpu.SemaphoreType.DMA((planes // FETCHED,)),
            pltpu.VMEM((groups, GROUP * slab_rows, cols), jnp.bfloat16),
            pltpu.VMEM((groups, BLOCKS * slab_rows, GROUP * slab_rows), jnp.bfloat16),
            pltpu.VMEM((GROUP, run_cols), jnp.int32),
            pltpu.VMEM((GROUP, run_cols), jnp.float32),
            pltpu.VMEM((GROUP, run_cols), jnp.float32),
        ],
        compiler_params=PARAMS,
        name="forward_planes",
    )(magnify, volume)


def backward(magnify, residual, halo):
    planes = magnify.shape[0]
    slab_rows, cols = residual.shape
    run_cols = cols + LANES
    shape = (planes, slab_rows, cols)
    return pl.pallas_call(
        backward_kernel,
        in_specs=[SMEM, VMEM, VMEM],
        out_specs=ANY,
        out_shape=jax.ShapeDtypeStruct(shape, jnp.bfloat16),
        scratch_shapes=[
            pltpu.VMEM(shape, jnp.bfloat16),
            pltpu.SemaphoreType.DMA((planes // SENT,)),
            pltpu.VMEM((LANES, cols), jnp.bfloat16),
            pltpu.VMEM((planes * slab_rows, LANES), jnp.bfloat16),
            pltpu.VMEM((planes * slab_rows, run_cols), jnp.bfloat16),
            pltpu.VMEM((GROUP, run_cols), jnp.int32),
            pltpu.VMEM((GROUP, run_cols), jnp.float32),
            pltpu.VMEM((GROUP, run_cols), jnp.float32),
            pltpu.VMEM((GROUP, run_cols), jnp.float32),
        ],
        compiler_params=PARAMS,
        name="backward_planes",
    )(magnify, residual, halo)


def reaches(slab, other, slab_rows, rows_all):
    half = rows_all / 2
    spread = (REACH * slab_rows - 3.0) / (half + 1.0)
    least, most = slab * slab_rows - 1.1, (slab + 1) * slab_rows + 0.1
    for detector in range(other * slab_rows, (other + 1) * slab_rows):
        from_middle = detector + 0.5 - half
        ends = (from_middle / (1.0 - spread), from_middle / (1.0 + spread))
        if max(ends) + half - 0.5 > least and min(ends) + half - 0.5 < most:
            return True
    return False


def both_ways(block, distance, samples):
    slab_rows = block.shape[0]
    slabs, members = lax.axis_size("slab"), lax.axis_size("row")
    route = []
    for s in range(slabs):
        for q in range(members):
            to = s + (distance if q % 2 == 0 else -distance)
            if 0 <= to < slabs:
                rows_of, block_of = (s, to) if samples else (to, s)
                if reaches(rows_of, block_of, slab_rows, slab_rows * slabs):
                    route.append((s * members + q, to * members + q))
    return lax.ppermute(block, ("slab", "row"), route)


def shards(volume, magnify, goal, live_pixels):
    slab_rows, own_cols = goal.shape
    row_count = lax.axis_size("row")
    cols = own_cols * row_count

    pairs = [[q, q + 1] for q in range(0, row_count, 2)]
    across = [[q, q + 2] for q in range(row_count // 2)]
    own, near, far, send = forward(magnify, volume)
    sent = lax.all_gather(send, "row", axis_index_groups=pairs)
    got = jnp.where(lax.axis_index("row") % 2 == 0, sent[1], sent[0]).astype(jnp.float32)
    near = both_ways((near + got[:slab_rows]).astype(jnp.bfloat16), 1, True)
    far = both_ways((far + got[slab_rows:]).astype(jnp.bfloat16), 2, True)
    total = own + near.astype(jnp.float32) + far.astype(jnp.float32)

    coarse = goal.astype(jnp.bfloat16)
    fine = (goal - coarse.astype(jnp.float32)).astype(jnp.bfloat16)
    coarse = jnp.where(live_pixels == 0, jnp.bfloat16(DEAD), coarse)
    message = jnp.concatenate([total.astype(jnp.bfloat16), coarse, fine], axis=1)
    halves = lax.all_gather(message, "row", axis_index_groups=across)
    total = halves[0, :, :cols].astype(jnp.float32) + halves[1, :, :cols].astype(jnp.float32)
    message = jnp.concatenate(
        [total.astype(jnp.bfloat16), halves[0, :, cols:], halves[1, :, cols:]], axis=1
    )
    gathered = lax.all_gather(message, "row", axis_index_groups=pairs).astype(jnp.float32)
    projection = gathered[0, :, :cols] + gathered[1, :, :cols]
    members = [
        gathered[core, :, cols + 2 * half * own_cols : cols + 2 * (half + 1) * own_cols]
        for half in range(2)
        for core in range(2)
    ]
    all_coarse = jnp.concatenate([member[:, :own_cols] for member in members], axis=1)
    all_fine = jnp.concatenate([member[:, own_cols:] for member in members], axis=1)
    residual = jnp.where(
        all_coarse > 0.5 * DEAD, 0.0, projection - (all_coarse + all_fine)
    ).astype(jnp.bfloat16)
    own_projection = lax.dynamic_slice_in_dim(
        projection, lax.axis_index("row") * own_cols, own_cols, axis=1
    )

    arrived = jnp.concatenate([both_ways(residual, 1, False), both_ways(residual, 2, False)], axis=0)
    halo = lax.all_gather(arrived, "row", axis_index_groups=pairs)
    return (own_projection, backward(magnify, residual, halo))


def solution(mesh):
    in_specs = (P("row", "slab", None), P("row"), P("slab", "row"), P("slab", "row"))
    out_specs = (P("slab", "row"), P("row", "slab", None))
    return jax.shard_map(shards, mesh=mesh, in_specs=in_specs, out_specs=out_specs, check_vma=False)
```

```python
import jax
import jax.numpy as jnp
from jax import lax
from jax.experimental import pallas as pl
from jax.experimental.pallas import tpu as pltpu
from jax.sharding import PartitionSpec as P

REACH = 2
BLOCKS = 2 * REACH + 1
LANES = 128
LANE_BITS = 7
FIXED_BITS = 16
FIXED = float(1 << FIXED_BITS)
GROUP = 8
SENT = 2
FETCHED = 8
RUN = 121
DEAD = 1e30

LANE_GATHER = lax.GatherDimensionNumbers(
    offset_dims=(),
    collapsed_slice_dims=(1,),
    start_index_map=(1,),
    operand_batching_dims=(0,),
    start_indices_batching_dims=(0,),
)


def pick(block, lanes):
    return lax.gather(
        block,
        lanes[..., None],
        LANE_GATHER,
        (1, 1),
        mode=lax.GatherScatterMode.PROMISE_IN_BOUNDS,
    )


def window(start, ref, rows):
    block = pl.multiple_of((start >> LANE_BITS) * LANES, LANES)
    one = ref[rows + (pl.ds(block, LANES),)]
    two = ref[rows + (pl.ds(block + LANES, LANES),)]
    lane = lax.broadcasted_iota(jnp.int32, one.shape, 1).astype(jnp.int16)
    edge = jnp.full(one.shape, start & (LANES - 1), jnp.int32).astype(jnp.int16)
    return jnp.where(lane >= edge, one, two)


def joined(group, before, after):
    lane = lax.broadcasted_iota(jnp.int32, before.shape, 1).astype(jnp.int16)
    return jnp.where(lane < RUN - (LANES - RUN) * group, before, after)


def run_columns(group, lane):
    return lane + jnp.where(lane >= LANES - (LANES - RUN) * group, group - 1, group) * LANES


def run_starts(first, stride, last):
    at = (first * FIXED).astype(jnp.int32)
    step = (stride * FIXED).astype(jnp.int32)
    while True:
        yield jnp.clip(at >> FIXED_BITS, 0, last)
        at = at + step


def factors_on_sublanes(magnify_ref, first):
    plane = lax.broadcasted_iota(jnp.int32, (GROUP, LANES), 0)
    factors = jnp.full((GROUP, LANES), magnify_ref[first], jnp.float32)
    for i in range(1, GROUP):
        factors = jnp.where(plane == i, magnify_ref[first + i], factors)
    return factors


def rounded(weights):
    return weights.astype(jnp.bfloat16).astype(jnp.float32)


def interpolated(values, lanes, weights):
    total = None
    for step, weight in enumerate(weights):
        picked = pick(values, (lanes + step) & (LANES - 1) if step else lanes)
        term = picked.astype(jnp.float32) * weight
        total = term if total is None else total + term
    return total.astype(values.dtype)


def forward_kernel(
    magnify_in, volume_ref, own_ref, near_ref, far_ref, send_ref,
    magnify_ref, noted, volume, arrival, resampled, row_table, source, low, high,
):
    planes, slab_rows, cols = volume_ref.shape
    groups = planes // GROUP
    half = cols // 2
    blocks = cols // LANES
    frame_rows = BLOCKS * slab_rows
    vol_first = lax.axis_index("slab") * slab_rows
    middle = slab_rows * lax.axis_size("slab") // 2

    def fetch(part):
        planes_of = pl.ds(part * FETCHED, FETCHED)
        return pltpu.make_async_copy(
            volume_ref.at[planes_of], volume.at[planes_of, :, pl.ds(0, cols)], arrival.at[part]
        )

    note = pltpu.make_async_copy(magnify_in, magnify_ref, noted)
    note.start()
    for part in range(planes // FETCHED):
        fetch(part).start()
    note.wait()

    lane = lax.broadcasted_iota(jnp.int32, (GROUP, LANES), 1)
    row = lax.broadcasted_iota(jnp.int32, (frame_rows, GROUP * slab_rows), 0)
    lane_id = lax.broadcasted_iota(jnp.int32, (frame_rows, GROUP * slab_rows), 1)
    detector = (row + (vol_first - REACH * slab_rows)).astype(jnp.float32) + (0.5 - middle)
    axial = ((lane_id & (slab_rows - 1)) + vol_first).astype(jnp.float32) - (middle - 0.5)

    def group_step(group, carry):
        first = group * GROUP
        factors = factors_on_sublanes(magnify_ref, first)
        for g in range(blocks + 1):
            column = run_columns(g, lane).astype(jnp.float32)
            at = (column + 0.5 - half) / factors + (half - 0.5)
            floor_at = jnp.floor(at)
            part = at - floor_at
            position = floor_at.astype(jnp.int32)
            here = slice(g * LANES, (g + 1) * LANES)
            source[:, here] = position & (LANES - 1)
            low[:, here] = jnp.where(
                (position >= 0) & (position < cols), rounded(1.0 - part), 0.0
            )
            high[:, here] = jnp.where(
                (position >= -1) & (position < cols - 1), rounded(part), 0.0
            )

        lane_factor = jnp.full(row.shape, magnify_ref[first], jnp.float32)
        for i in range(1, GROUP):
            lane_factor = jnp.where(lane_id >= i * slab_rows, magnify_ref[first + i], lane_factor)
        row_table[group] = jnp.maximum(
            0.0, 1.0 - jnp.abs(detector / lane_factor - axial)
        ).astype(jnp.bfloat16)

        for i in range(GROUP):
            rate = 1.0 / magnify_ref[first + i]
            starts = run_starts((0.5 - half) * rate + (half - 0.75), RUN * rate, cols - LANES)
            out_rows = slice(i * slab_rows, (i + 1) * slab_rows)
            if i % FETCHED == 0:
                fetch(group * (GROUP // FETCHED) + i // FETCHED).wait()
            before = None
            for g in range(blocks + 1):
                here = slice(g * LANES, (g + 1) * LANES)
                values = window(next(starts), volume, (first + i, slice(None)))
                lanes = jnp.broadcast_to(source[i : i + 1, here], values.shape).astype(jnp.int16)
                run = interpolated(
                    values, lanes, (low[i : i + 1, here], high[i : i + 1, here])
                )
                if before is not None:
                    resampled[group, out_rows, (g - 1) * LANES : g * LANES] = joined(
                        g - 1, before, run
                    )
                before = run
        return carry

    lax.fori_loop(0, groups, group_step, 0, unroll=True)

    upward = lax.axis_index("row") % 2 == 0
    r = slab_rows
    for c in range(0, cols, 512):
        here = slice(c, c + 512)
        frame = None
        for group in range(groups):
            part = jnp.dot(
                row_table[group], resampled[group, :, here], preferred_element_type=jnp.float32
            )
            frame = part if frame is None else frame + part
        own_ref[:, here] = frame[2 * r : 3 * r]
        near_ref[:, here] = jnp.where(upward, frame[3 * r : 4 * r], frame[r : 2 * r])
        far_ref[:, here] = jnp.where(upward, frame[4 * r :], frame[:r])
        send_ref[:r, here] = jnp.where(upward, frame[r : 2 * r], frame[3 * r : 4 * r]).astype(
            send_ref.dtype
        )
        send_ref[r:, here] = jnp.where(upward, frame[:r], frame[4 * r :]).astype(send_ref.dtype)


def backward_kernel(
    magnify_ref, own_ref, halo_ref, out_ref,
    out, departure, frame, row_table, smeared, source, weight0, weight1, weight2,
):
    planes, slab_rows, cols = out_ref.shape
    groups = planes // GROUP
    half = cols // 2
    blocks = cols // LANES
    vol_first = lax.axis_index("slab") * slab_rows
    middle = slab_rows * lax.axis_size("slab") // 2

    def store(part):
        planes_of = pl.ds(part * SENT, SENT)
        return pltpu.make_async_copy(out.at[planes_of], out_ref.at[planes_of], departure.at[part])

    r = slab_rows
    frame[:r, :] = halo_ref[0, r:, :]
    frame[r : 2 * r, :] = halo_ref[0, :r, :]
    frame[2 * r : 3 * r, :] = own_ref[...]
    frame[3 * r : 5 * r, :] = halo_ref[1]
    frame[5 * r :, :] = jnp.zeros((frame.shape[0] - 5 * r, cols), frame.dtype)

    row = lax.broadcasted_iota(jnp.int32, (slab_rows, LANES), 0)
    lane_id = lax.broadcasted_iota(jnp.int32, (slab_rows, LANES), 1)
    axial = (row + vol_first).astype(jnp.float32) - (middle - 0.5)
    detector = (lane_id + (vol_first - REACH * slab_rows)).astype(jnp.float32) + (0.5 - middle)
    for i in range(planes):
        row_table[i * r : (i + 1) * r, :] = jnp.maximum(
            0.0, 1.0 - jnp.abs(detector / magnify_ref[i] - axial)
        ).astype(jnp.bfloat16)
    for c in range(0, cols, 256):
        smeared[:, c : c + 256] = jnp.dot(
            row_table[...], frame[:, c : c + 256], preferred_element_type=jnp.float32
        ).astype(jnp.bfloat16)

    lane = lax.broadcasted_iota(jnp.int32, (GROUP, LANES), 1)

    def group_step(group, carry):
        first = group * GROUP
        factors = factors_on_sublanes(magnify_ref, first)
        for g in range(blocks + 1):
            target = run_columns(g, lane).astype(jnp.float32)
            tap = jnp.floor((target - (half + 0.5)) * factors + (half - 0.501)) + 1.0
            here = slice(g * LANES, (g + 1) * LANES)
            source[:, here] = tap.astype(jnp.int32) & (LANES - 1)
            for step, weight in enumerate((weight0, weight1, weight2)):
                column = tap + step
                at = (column + (0.5 - half)) / factors + (half - 0.5)
                weight[:, here] = jnp.where(
                    (column >= 0.0) & (column < cols),
                    rounded(jnp.maximum(0.0, 1.0 - jnp.abs(at - target))),
                    0.0,
                )

        for i in range(GROUP):
            factor = magnify_ref[first + i]
            starts = run_starts(
                (-half - 0.5) * factor + (half + 0.249), RUN * factor, cols - LANES
            )
            rows = (pl.ds(pl.multiple_of((first + i) * r, r), r),)
            before = None
            for g in range(blocks + 1):
                here = slice(g * LANES, (g + 1) * LANES)
                values = window(next(starts), smeared, rows)
                lanes = jnp.broadcast_to(source[i : i + 1, here], values.shape).astype(jnp.int16)
                run = interpolated(
                    values, lanes, [w[i : i + 1, here] for w in (weight0, weight1, weight2)]
                )
                if before is not None:
                    out[first + i, :, (g - 1) * LANES : g * LANES] = joined(g - 1, before, run)
                before = run
            if (i + 1) % SENT == 0:
                store(group * (GROUP // SENT) + i // SENT).start()
        return carry

    lax.fori_loop(0, groups, group_step, 0)
    for part in range(planes // SENT):
        store(part).wait()


PARAMS = pltpu.CompilerParams(vmem_limit_bytes=53 << 20)
SMEM = pl.BlockSpec(memory_space=pltpu.SMEM)
VMEM = pl.BlockSpec(memory_space=pltpu.VMEM)
ANY = pl.BlockSpec(memory_space=pl.ANY)


def forward(magnify, volume):
    planes, slab_rows, cols = volume.shape
    groups = planes // GROUP
    band = (slab_rows, cols)
    pair = (2 * slab_rows, cols)
    run_cols = cols + LANES
    return pl.pallas_call(
        forward_kernel,
        in_specs=[ANY, ANY],
        out_specs=[VMEM] * 4,
        out_shape=[jax.ShapeDtypeStruct(band, jnp.float32)] * 3
        + [jax.ShapeDtypeStruct(pair, jnp.bfloat16)],
        scratch_shapes=[
            pltpu.SMEM((planes,), jnp.float32),
            pltpu.SemaphoreType.DMA(()),
            pltpu.VMEM((planes, slab_rows, run_cols), volume.dtype),
            pltpu.SemaphoreType.DMA((planes // FETCHED,)),
            pltpu.VMEM((groups, GROUP * slab_rows, cols), jnp.bfloat16),
            pltpu.VMEM((groups, BLOCKS * slab_rows, GROUP * slab_rows), jnp.bfloat16),
            pltpu.VMEM((GROUP, run_cols), jnp.int32),
            pltpu.VMEM((GROUP, run_cols), jnp.float32),
            pltpu.VMEM((GROUP, run_cols), jnp.float32),
        ],
        compiler_params=PARAMS,
        name="forward_planes",
    )(magnify, volume)


def backward(magnify, residual, halo):
    planes = magnify.shape[0]
    slab_rows, cols = residual.shape
    run_cols = cols + LANES
    shape = (planes, slab_rows, cols)
    return pl.pallas_call(
        backward_kernel,
        in_specs=[SMEM, VMEM, VMEM],
        out_specs=ANY,
        out_shape=jax.ShapeDtypeStruct(shape, jnp.bfloat16),
        scratch_shapes=[
            pltpu.VMEM(shape, jnp.bfloat16),
            pltpu.SemaphoreType.DMA((planes // SENT,)),
            pltpu.VMEM((LANES, cols), jnp.bfloat16),
            pltpu.VMEM((planes * slab_rows, LANES), jnp.bfloat16),
            pltpu.VMEM((planes * slab_rows, run_cols), jnp.bfloat16),
            pltpu.VMEM((GROUP, run_cols), jnp.int32),
            pltpu.VMEM((GROUP, run_cols), jnp.float32),
            pltpu.VMEM((GROUP, run_cols), jnp.float32),
            pltpu.VMEM((GROUP, run_cols), jnp.float32),
        ],
        compiler_params=PARAMS,
        name="backward_planes",
    )(magnify, residual, halo)


def reaches(slab, other, slab_rows, rows_all):
    half = rows_all / 2
    spread = (REACH * slab_rows - 3.0) / (half + 1.0)
    least, most = slab * slab_rows - 1.1, (slab + 1) * slab_rows + 0.1
    for detector in range(other * slab_rows, (other + 1) * slab_rows):
        from_middle = detector + 0.5 - half
        ends = (from_middle / (1.0 - spread), from_middle / (1.0 + spread))
        if max(ends) + half - 0.5 > least and min(ends) + half - 0.5 < most:
            return True
    return False


def both_ways(block, distance, samples):
    slab_rows = block.shape[0]
    slabs, members = lax.axis_size("slab"), lax.axis_size("row")
    route = []
    for s in range(slabs):
        for q in range(members):
            to = s + (distance if q % 2 == 0 else -distance)
            if 0 <= to < slabs:
                rows_of, block_of = (s, to) if samples else (to, s)
                if reaches(rows_of, block_of, slab_rows, slab_rows * slabs):
                    route.append((s * members + q, to * members + q))
    return lax.ppermute(block, ("slab", "row"), route)


def shards(volume, magnify, goal, live_pixels):
    slab_rows, own_cols = goal.shape
    row_count = lax.axis_size("row")
    cols = own_cols * row_count

    pairs = [[q, q + 1] for q in range(0, row_count, 2)]
    across = [[q, q + 2] for q in range(row_count // 2)]
    own, near, far, send = forward(magnify, volume)
    sent = lax.all_gather(send, "row", axis_index_groups=pairs)
    got = jnp.where(lax.axis_index("row") % 2 == 0, sent[1], sent[0]).astype(jnp.float32)
    near = both_ways((near + got[:slab_rows]).astype(jnp.bfloat16), 1, True)
    far = both_ways((far + got[slab_rows:]).astype(jnp.bfloat16), 2, True)
    total = own + near.astype(jnp.float32) + far.astype(jnp.float32)

    coarse = goal.astype(jnp.bfloat16)
    fine = (goal - coarse.astype(jnp.float32)).astype(jnp.bfloat16)
    coarse = jnp.where(live_pixels == 0, jnp.bfloat16(DEAD), coarse)
    message = jnp.concatenate([total.astype(jnp.bfloat16), coarse, fine], axis=1)
    halves = lax.all_gather(message, "row", axis_index_groups=across)
    total = halves[0, :, :cols].astype(jnp.float32) + halves[1, :, :cols].astype(jnp.float32)
    message = jnp.concatenate(
        [total.astype(jnp.bfloat16), halves[0, :, cols:], halves[1, :, cols:]], axis=1
    )
    gathered = lax.all_gather(message, "row", axis_index_groups=pairs).astype(jnp.float32)
    projection = gathered[0, :, :cols] + gathered[1, :, :cols]
    members = [
        gathered[core, :, cols + 2 * half * own_cols : cols + 2 * (half + 1) * own_cols]
        for half in range(2)
        for core in range(2)
    ]
    all_coarse = jnp.concatenate([member[:, :own_cols] for member in members], axis=1)
    all_fine = jnp.concatenate([member[:, own_cols:] for member in members], axis=1)
    residual = jnp.where(
        all_coarse > 0.5 * DEAD, 0.0, projection - (all_coarse + all_fine)
    ).astype(jnp.bfloat16)
    own_projection = lax.dynamic_slice_in_dim(
        projection, lax.axis_index("row") * own_cols, own_cols, axis=1
    )

    arrived = jnp.concatenate([both_ways(residual, 1, False), both_ways(residual, 2, False)], axis=0)
    halo = lax.all_gather(arrived, "row", axis_index_groups=pairs)
    return (own_projection, backward(magnify, residual, halo))


def solution(mesh):
    in_specs = (P("row", "slab", None), P("row"), P("slab", "row"), P("slab", "row"))
    out_specs = (P("slab", "row"), P("row", "slab", None))
    return jax.shard_map(shards, mesh=mesh, in_specs=in_specs, out_specs=out_specs, check_vma=False)
```
